32 devices in a mesh: dp: 4 (over y, x), brick: 8 (over z, core).
Axes of the slice: x: 2, y: 2, z: 4, core: 2. Of those that a mesh axis runs over, the one named last changes fastest.
Arguments:
- features: bfloat16 [4, 64, 512, 64], P('dp', 'brick'), may hold values from -6 to 6
- occupancy: int32 [4, 64, 512], P('dp', 'brick'), may hold values 0 or 1
- neighbours: int32 [4, 64, 27], P('dp', 'brick'), may hold values from -1 to 63, as said below
- owners: int32 [4, 64], P('dp', 'brick'), may hold values from 0 to 63, as said below
- w_conv: bfloat16 [3, 3, 3, 64, 64], replicated, may hold values from -0.15625 to 0.15625
- w_down: bfloat16 [2, 2, 2, 64, 128], replicated, may hold values from -0.25 to 0.25
- w_point: bfloat16 [128, 256], replicated, may hold values from -0.5 to 0.5
- cotangent: bfloat16 [4, 64, 64, 256], P('dp', 'brick'), may hold values from -0.046875 to 0.046875
Outputs:
- grad_w_conv: float32 [3, 3, 3, 64, 64], replicated
- grad_w_down: float32 [2, 2, 2, 64, 128], replicated
- grad_w_point: float32 [128, 256], replicated
The draws below stay inside these ranges and needn't reach their ends.
Inputs may be any that keep to these rules, and one draw needn't show every extreme that they name: `neighbours`: bricks of a scene form a lattice of 16 x 4 x 1 bricks, 8 consecutive ids a device; an entry names the lattice neighbour at its column's offset or is -1; column 13 is the brick itself. Columns with first offset 0 name bricks of the same device, offset -1 of the same or the previous device, offset +1 of the same or the next. `owners`: within a scene a permutation of the coarse slots; a slot's device is slot // 8. A device hands exactly 1 bricks to each device it hands any to.
All inputs are finite; a program needn't handle non-finite values. No bound on the sum of `occupancy` on one device may be relied on, other than what follows from the above.
Results may differ from the reference program's by a relative error of at most 0.012.
Values may be sent and summed in bfloat16 or wider, within the bound.
No kernel may reach another device: no remote copies, remote signals or barrier semaphores. Data moves between devices by JAX's collectives and lax.ppermute only.
A program may use at most 64 MiB of HBM per device.

```python
import jax
import jax.numpy as jnp
from jax import lax

C0 = 64
C1 = 128
C2 = 256
BY = 4
BZ = 1
NB = 8
NBT = 64
N_DP = 4
N_BRICK = 8


def draw_neighbours(key, part):
    cells = jnp.arange(NBT, dtype=jnp.int32)
    device_of = cells // NB
    inner = cells % NB
    xpos = device_of * 2 + inner // (BY * BZ)
    ypos = inner // BZ % BY
    zpos = inner % BZ
    columns = []
    for a in range(3):
        for b in range(3):
            for c in range(3):
                near_x = xpos + a - 1
                near_y = ypos + b - 1
                near_z = zpos + c - 1
                inside = (near_x >= 0) & (near_x < 2 * N_BRICK) & (near_y >= 0) & (near_y < BY) & (near_z >= 0) & (near_z < BZ)
                ident = near_x // 2 * NB + near_x % 2 * (BY * BZ) + near_y * BZ + near_z
                columns.append(jnp.where(inside, ident, -1))
    lattice = jnp.stack(columns, axis=1)
    keep = jax.random.randint(jax.random.fold_in(key, 3), (N_DP, NBT, 27), 0, 4) > 0
    centre = (jnp.arange(27) == 13)[None, None, :]
    return jnp.where(keep | centre, lattice[None], -1).astype(jnp.int32)


def place_value(order, where, wanted):
    found = jnp.argmax(order == wanted).astype(jnp.int32)
    held = order[where]
    return order.at[found].set(held).at[where].set(wanted)


def permute_bricks(subkey):
    order = jax.random.permutation(subkey, N_BRICK).astype(jnp.int32)
    order = place_value(order, 0, N_BRICK // 2)
    order = place_value(order, 1, 1)
    order = place_value(order, 2, N_BRICK - 1)
    return order


def permute_slots(subkey):
    return jax.random.permutation(subkey, NB)


def draw_owners(key, part):
    shift_keys = jax.random.split(jax.random.fold_in(key, 7), N_DP)
    shifts = jax.vmap(permute_bricks)(shift_keys)
    slot_keys = jax.random.split(jax.random.fold_in(key, 11), N_DP * N_BRICK)
    orders = jax.vmap(permute_slots)(slot_keys).reshape(N_DP, N_BRICK, NB)
    inner = jnp.arange(NB, dtype=jnp.int32)
    offsets = shifts[:, inner % N_BRICK]
    source = jnp.arange(N_BRICK, dtype=jnp.int32)[None, :, None]
    dest_dev = (source + offsets[:, None, :]) % N_BRICK
    group = jnp.arange(N_DP, dtype=jnp.int32)[:, None, None]
    slots_at = orders[group, dest_dev, inner[None, None, :]]
    return (dest_dev * NB + slots_at).reshape(N_DP, NBT).astype(jnp.int32)


def touch_ends(drawn, stream_key, smallest, top_value):
    extent = drawn.shape
    index_at = [jax.random.randint(jax.random.fold_in(stream_key, axis), (), 0, extent[axis]) for axis in range(len(extent))]
    drawn = drawn.at[tuple(index_at)].set(smallest)
    longest = extent.index(max(extent))
    index_at[longest] = (index_at[longest] + 1) % extent[longest]
    return drawn.at[tuple(index_at)].set(top_value)


def block_scale(rng, dims, cuts, low, high):
    factor_of = 1.0
    for dim, parts in cuts:
        steps = jax.random.uniform(jax.random.fold_in(jax.random.fold_in(rng, 6), dim), (parts,), jnp.float32, low / len(cuts), high / len(cuts))
        factor_of = factor_of * jnp.repeat(jnp.exp(steps), dims[dim] // parts).reshape((-1,) + (1,) * (len(dims) - 1 - dim))
    return factor_of


def bell_draw(stream_key, shape, deviation, reach, cuts=(), held_as=jnp.bfloat16):
    values = deviation * jax.random.normal(stream_key, shape, jnp.float32)
    if cuts:
        values = values * block_scale(stream_key, shape, cuts, -0.22, 0.18)
    return jnp.clip(values, -reach, reach).astype(held_as)


def setup_inputs(seed: int = 0) -> dict:
    keys = jax.random.split(jax.random.key(seed), 9)
    features = bell_draw(keys[0], (N_DP, NBT, 512, C0), 1.0, 6.0, ((0, 4), (1, 8)))
    occupancy = touch_ends((jax.random.randint(keys[1], (N_DP, NBT, 512), 0, 4) < 3).astype(jnp.int32), jax.random.fold_in(keys[1], 1), 0, 1)
    neighbours = draw_neighbours(jax.random.fold_in(keys[8], 71), 0)
    owners = draw_owners(jax.random.fold_in(keys[8], 71), 0)
    w_conv = bell_draw(keys[4], (3, 3, 3, C0, C0), (27 * C0) ** -0.5, 0.15625)
    w_down = bell_draw(keys[5], (2, 2, 2, C0, C1), (8 * C0) ** -0.5, 0.25)
    w_point = bell_draw(keys[6], (C1, C2), C1 ** -0.5, 0.5)
    cotangent = bell_draw(keys[7], (N_DP, NBT, 64, C2), ((N_DP * NBT * 64) ** -0.5), 0.046875, ((0, 4), (1, 8)))
    return dict(features=features, occupancy=occupancy, neighbours=neighbours, owners=owners, w_conv=w_conv, w_down=w_down, w_point=w_point, cotangent=cotangent)


SPANS = ((7, 8), (0, 8), (0, 1))


def assemble(pools, indices):
    planes = []
    for a in range(3):
        row_parts = []
        for b in range(3):
            col_parts = []
            for c in range(3):
                window_part = pools[a][:, :, SPANS[b][0]:SPANS[b][1], SPANS[c][0]:SPANS[c][1], :]
                col_parts.append(jnp.take(window_part, indices[a][:, 9 * a + 3 * b + c], axis=0, mode="clip"))
            row_parts.append(jnp.concatenate(col_parts, axis=3))
        planes.append(jnp.concatenate(row_parts, axis=2))
    return jnp.concatenate(planes, axis=1)


def silu_slope(signal):
    gate_value = jax.nn.sigmoid(signal)
    return gate_value * (1.0 + signal * (1.0 - gate_value))


def one_group(features, occupancy, neighbours, owners, w_conv, w_down, w_point, cotangent):
    brick_count = features.shape[0]
    in_width = features.shape[2]
    mid_width = w_point.shape[0]
    highest = lax.Precision.HIGHEST
    bricks = features.reshape(brick_count, 8, 8, 8, in_width)
    brick_pool = jnp.concatenate([bricks, jnp.zeros((1, 8, 8, 8, in_width), bricks.dtype)], axis=0)
    pool_index = jnp.where(neighbours >= 0, neighbours, brick_count).astype(jnp.int32)
    padded = assemble((brick_pool[:, 7:8], brick_pool, brick_pool[:, 0:1]), (pool_index, pool_index, pool_index))
    pre_act = lax.conv_general_dilated(padded.astype(jnp.float32), w_conv.astype(jnp.float32), (1, 1, 1), "VALID", dimension_numbers=("NDHWC", "DHWIO", "NDHWC"), precision=highest)
    occupied = occupancy.reshape(brick_count, 8, 8, 8, 1).astype(jnp.float32)
    hidden = (jax.nn.silu(pre_act) * occupied).astype(jnp.bfloat16)
    grouped = hidden.reshape(brick_count, 4, 2, 4, 2, 4, 2, in_width)
    down_act = jnp.einsum("bpiqjrkc,ijkcd->bpqrd", grouped.astype(jnp.float32), w_down.astype(jnp.float32), precision=highest)
    coarse = jax.nn.silu(down_act).astype(jnp.bfloat16).reshape(brick_count, -1)
    placed = jnp.zeros_like(coarse).at[owners].set(coarse)
    row_block = placed.reshape(-1, mid_width)
    point_act = jnp.dot(row_block, w_point, preferred_element_type=jnp.float32)
    grad_point = (cotangent.reshape(point_act.shape).astype(jnp.float32) * silu_slope(point_act)).astype(jnp.bfloat16)
    grad_w_point = jnp.dot(row_block.T, grad_point, preferred_element_type=jnp.float32)
    grad_placed = jnp.dot(grad_point, w_point.T, preferred_element_type=jnp.float32).astype(jnp.bfloat16)
    grad_coarse = grad_placed.reshape(brick_count, -1)[owners]
    grad_down = (grad_coarse.reshape(down_act.shape).astype(jnp.float32) * silu_slope(down_act)).astype(jnp.bfloat16)
    grad_w_down = jnp.einsum("bpiqjrkc,bpqrd->ijkcd", grouped.astype(jnp.float32), grad_down.astype(jnp.float32), precision=highest)
    grad_hidden = jnp.einsum("bpqrd,ijkcd->bpiqjrkc", grad_down.astype(jnp.float32), w_down.astype(jnp.float32), precision=highest)
    grad_hidden = grad_hidden.reshape(brick_count, 8, 8, 8, in_width)
    grad_pre = (grad_hidden * occupied * silu_slope(pre_act)).astype(jnp.bfloat16)
    flat_grad = grad_pre.reshape(-1, in_width).astype(jnp.float32)
    term_list = []
    for a in range(3):
        for b in range(3):
            for c in range(3):
                window_part = padded[:, a:a + 8, b:b + 8, c:c + 8, :].reshape(-1, in_width).astype(jnp.float32)
                term_list.append(jnp.dot(window_part.T, flat_grad, precision=highest))
    grad_w_conv = jnp.stack(term_list).reshape(3, 3, 3, in_width, in_width)
    return grad_w_conv, grad_w_down, grad_w_point


def reference(features, occupancy, neighbours, owners, w_conv, w_down, w_point, cotangent):
    totals = None
    for group in range(N_DP):
        result = one_group(features[group], occupancy[group], neighbours[group], owners[group], w_conv, w_down, w_point, cotangent[group])
        if totals is None:
            totals = result
        else:
            totals = tuple(left + right for left, right in zip(totals, result))
    return (totals[0], totals[1], totals[2])
```

```python
import jax
import jax.numpy as jnp
from jax import lax
from jax.experimental import pallas as pl
from jax.experimental.pallas import tpu as pltpu
from jax.sharding import PartitionSpec as P

F32 = jnp.float32
BF16 = jnp.bfloat16
LANES = 128
VMEM = pl.BlockSpec(memory_space=pltpu.VMEM)
SMEM = pl.BlockSpec(memory_space=pltpu.SMEM)
CONV_ROWS, DOWN_ROWS, POINT_ROWS = 14 * 64, 512, 256
WIRE_ROWS = CONV_ROWS + DOWN_ROWS + POINT_ROWS
HALF = WIRE_ROWS // 2


def mm(a, b, ca=1, cb=0):
    return lax.dot_general(a, b, (((ca,), (cb,)), ((), ())), preferred_element_type=F32)


def sigmoid(v):
    return 1.0 / (1.0 + jnp.exp(-v))


def forward_kernel(
    feat, occ, valid, before, after, w4, wd, wp,
    shifted, slope_pre, hid, coarse_ref, slope_down, slope_point,
    planes, wide,
):
    lane = lax.broadcasted_iota(jnp.int32, (1, 512), 1)
    jj, kk, bb, qq, rr = lane // 256, lane // 128 % 2, lane % 128 // 16, lane // 4 % 4, lane % 4
    voxel = bb * 128 + 8 * (2 * qq + jj) + 2 * rr + kk
    row = lax.broadcasted_iota(jnp.int32, (1024, 512), 0)
    occ_f = occ[...].astype(F32).astype(BF16)
    rows = []
    for m in range(4):
        rows.append(jnp.concatenate([feat[b, :, 128 * m : 128 * m + 128] for b in range(8)], axis=1))
    occ_rows = [
        jnp.concatenate([occ_f[b : b + 1, 128 * m : 128 * m + 128] for b in range(8)], axis=1)
        for m in range(4)
    ]
    occ_rows = jnp.concatenate(occ_rows + [jnp.zeros((12, 1024), BF16)], axis=0)
    stacked = jnp.concatenate(rows + [occ_rows], axis=0)
    zero4 = jnp.zeros((64, 512), BF16)
    lower = jnp.concatenate([zero4] + [before[b] for b in range(4)], axis=1)
    upper = jnp.concatenate([after[b] for b in range(4)] + [zero4], axis=1)
    occ_x = [None] * 8
    edge = [None, None]
    for e in range(2):
        select = jnp.where(row == voxel + 64 * e, 1.0, 0.0).astype(BF16)
        other = upper if e == 0 else lower
        picked = mm(jnp.concatenate([stacked, other], axis=0), select)
        for m in range(4):
            planes[64 * (2 * m + e + 1) : 64 * (2 * m + e + 2), :] = picked[64 * m : 64 * m + 64]
            occ_x[2 * m + e] = picked[256 + m : 257 + m]
        edge[e] = picked[272:336]
    inner_x = lax.broadcasted_iota(jnp.int32, (64, 128), 1) >= 64
    for g in range(4):
        cut = slice(128 * g, 128 * g + 128)
        low = jnp.where(inner_x, edge[1][:, cut], planes[512:576, cut])
        planes[0:64, cut] = pltpu.roll(low, 64, 1)
        high = jnp.where(inner_x, planes[64:128, cut], edge[0][:, cut])
        planes[576:640, cut] = pltpu.roll(high, 64, 1)
    cell = lax.broadcasted_iota(jnp.int32, (1, 128), 1)
    q_at, r_at = cell // 4 % 4, cell % 4
    source = ((1, -1), (0, 0), (1, 0), (0, 1))
    for t in range(4):
        j, dq = source[t]
        for u in range(4):
            k, dr = source[u]
            g = 2 * j + k
            block = planes[:, 128 * g : 128 * g + 128]
            shift = -(4 * dq + dr) % 128
            if shift:
                block = pltpu.roll(block, shift, 1)
            if dr:
                inside = jnp.where(r_at + dr < 0, 0.0, jnp.where(r_at + dr > 3, 0.0, 1.0))
            else:
                inside = jnp.ones((1, 128), F32)
            cross = None if dq == 0 else (q_at == 0 if dq < 0 else q_at == 3)
            for a, (lo, hi) in enumerate(((0, 64), (64, 576), (576, 640))):
                keep = inside
                near = valid[9 * a + 4 : 9 * a + 5]
                if cross is not None:
                    col = 9 * a + 3 * (dq + 1) + 1
                    keep = keep * jnp.where(cross, valid[col : col + 1], near)
                elif a != 1:
                    keep = keep * near
                part = block[lo:hi]
                if a != 1 or dq or dr:
                    part = part * keep
                shifted[t, lo:hi, 128 * u : 128 * u + 128] = part.astype(BF16)
    zero = jnp.zeros((64, 128), BF16)
    for n in range(9):
        wa, wb, wc, wdd = (w4[n, i] for i in range(4))
        for x, parts in enumerate(((wa, wb, zero), (wc, wdd, zero), (zero, wa, wb), (zero, wc, wdd))):
            for i, part in enumerate(parts):
                wide[64 * x : 64 * x + 64, 384 * n + 128 * i : 384 * n + 128 * i + 128] = part
    for h in range(2):
        for j in range(2):
            taps = [
                shifted[j + b, 256 * h : 256 * h + 384, 128 * c : 128 * c + 256]
                for b in range(3)
                for c in range(3)
            ]
            pre = mm(wide[...], jnp.concatenate(taps, axis=0))
            gate = sigmoid(pre)
            for x in range(4):
                sub = slice(64 * x, 64 * x + 64)
                filled = occ_x[4 * h + x][:, 256 * j : 256 * j + 256]
                act, g = pre[sub], gate[sub]
                r0 = 256 * h + 64 * x
                slope_pre[r0 : r0 + 64, 256 * j : 256 * j + 256] = filled * (g * (1.0 + act * (1.0 - g)))
                out = (act * g * filled).astype(BF16)
                p, i = 2 * h + x // 2, x % 2
                for k in range(2):
                    base = 128 * (2 * j + k) + 64 * i
                    hid[base : base + 64, 128 * p : 128 * p + 128] = out[:, 128 * k : 128 * k + 128]
    down = mm(wd[...], hid[...], 0, 0)
    gate = sigmoid(down)
    coarse = (down * gate).astype(BF16)
    coarse_ref[...] = coarse
    slope_down[...] = gate * (1.0 + down * (1.0 - gate))
    point = mm(coarse, wp[...], 0, 0)
    gate = sigmoid(point)
    slope_point[...] = gate * (1.0 + point * (1.0 - gate))


def backward_kernel(
    where_from, core, shifted, slope_pre, hid, coarse, slope_down, slope_point, cot, wd, wp, wire, grads,
):
    def put(first, value):
        done = 0
        while done < value.shape[0]:
            half, at = divmod(first + done, HALF)
            size = min(value.shape[0] - done, HALF - at)
            wire[core[0] if half == 0 else 1 - core[0], at : at + size] = value[done : done + size].astype(BF16)
            done += size

    parts = []
    for p in range(4):
        for b in range(8):
            parts.append(cot[where_from[b], 16 * p : 16 * p + 16, :])
    cot_rows = jnp.concatenate(parts, axis=0)
    grad_point = (cot_rows.astype(F32) * slope_point[...]).astype(BF16)
    gwp = mm(coarse[...], grad_point)
    put(CONV_ROWS + DOWN_ROWS, jnp.concatenate([gwp[:, :128], gwp[:, 128:]], axis=0))
    grad_coarse = mm(wp[...], grad_point, 1, 1).astype(BF16)
    grad_down = (grad_coarse.astype(F32) * slope_down[...]).astype(BF16)
    put(CONV_ROWS, mm(hid[...], grad_down, 1, 1))
    for jk in range(4):
        grad_hidden = mm(wd[128 * jk : 128 * jk + 128], grad_down)
        for p in range(4):
            cut = slice(128 * jk, 128 * jk + 128)
            value = grad_hidden[:, 128 * p : 128 * p + 128] * slope_pre[128 * p : 128 * p + 128, cut]
            h, base = p // 2, 128 * (p % 2)
            grads[base : base + 128, 512 * h + 128 * jk : 512 * h + 128 * jk + 128] = value.astype(BF16)
    low_lanes = lax.broadcasted_iota(jnp.int32, (64, 128), 1) < 64
    thirds = []
    for n in range(9):
        b, c = divmod(n, 3)
        left = jnp.concatenate(
            [
                shifted[j + b, 256 * h : 256 * h + 384, 128 * c : 128 * c + 256]
                for h in range(2)
                for j in range(2)
            ],
            axis=1,
        )
        band = mm(left, grads[...], 1, 1)
        sums = []
        for a in range(3):
            even = band[64 * a : 64 * a + 64, :128] + band[64 * a + 128 : 64 * a + 192, 128:]
            odd = band[64 * a + 64 : 64 * a + 128, :128] + band[64 * a + 192 : 64 * a + 256, 128:]
            both = jnp.where(low_lanes, even, odd)
            sums.append(both + pltpu.roll(both, 64, 1))
        put(64 * n, jnp.where(low_lanes, sums[0], sums[1]))
        thirds.append(sums[2])
    for n in range(5):
        put(64 * (9 + n), jnp.where(low_lanes, thirds[2 * n], thirds[min(2 * n + 1, 8)]))


def finish_kernel(core, mine, other, gwc, gwd, gwp, total):
    total[core[0]] = mine[...]
    total[1 - core[0]] = other[...]

    def rows(first, count):
        half, at = divmod(first, HALF)
        if at + count <= HALF:
            return total[half, at : at + count]
        cut = HALF - at
        return jnp.concatenate([total[half, at:], total[half + 1, : count - cut]], axis=0)

    for n in range(9):
        pair = rows(64 * n, 64).astype(F32)
        gwc[n] = pair[:, :64]
        gwc[9 + n] = pair[:, 64:]
    for n in range(5):
        pair = rows(64 * (9 + n), 64).astype(F32)
        gwc[18 + 2 * n] = pair[:, :64]
        if n < 4:
            gwc[19 + 2 * n] = pair[:, 64:]
    for i in range(2):
        for jk in range(4):
            gwd[4 * i + jk] = rows(CONV_ROWS + 128 * jk + 64 * i, 64).astype(F32)
    for s in range(2):
        gwp[:, 128 * s : 128 * s + 128] = rows(CONV_ROWS + DOWN_ROWS + 128 * s, 128).astype(F32)


def call(kernel, outs, ins, scratch=(), limit=24 * 2**20, flops=0, specs=None):
    return pl.pallas_call(
        kernel,
        out_shape=outs,
        in_specs=specs or [VMEM] * len(ins),
        out_specs=jax.tree.map(lambda _: VMEM, outs),
        scratch_shapes=scratch,
        compiler_params=pltpu.CompilerParams(vmem_limit_bytes=limit),
        cost_estimate=pl.CostEstimate(flops=flops, bytes_accessed=2**20, transcendentals=0),
    )(*ins)


def swap(value, axis, bit):
    size = lax.axis_size(axis)
    return lax.ppermute(value, axis, [(i, i ^ bit) for i in range(size)])


def powers(size, first):
    bits = []
    while first < size:
        bits.append(first)
        first *= 2
    return bits


def shards(features, occupancy, neighbours, owners, w_conv, w_down, w_point, cotangent):
    dp_size, brick_size = lax.axis_size("dp"), lax.axis_size("brick")
    core = (lax.axis_index("brick") % 2).astype(jnp.int32).reshape(1)
    feat = jnp.swapaxes(features[0], 1, 2)
    slots = owners[0]
    target = slots // 8
    wanted = jnp.arange(brick_size, dtype=jnp.int32)[:, None] == target[None, :]
    request = jnp.max(jnp.where(wanted, (slots % 8)[None, :], 0), axis=1)
    arrived = lax.all_to_all(request, "brick", split_axis=0, concat_axis=0, tiled=True)
    reply = jnp.take(cotangent[0], arrived, axis=0, mode="clip")
    fetched = lax.all_to_all(reply, "brick", split_axis=0, concat_axis=0, tiled=True)
    up = [(i, i + 1) for i in range(brick_size - 1)]
    down = [(j, i) for i, j in up]
    before = lax.ppermute(feat[4:8, :, 384:512], "brick", up)
    after = lax.ppermute(feat[0:4, :, 0:128], "brick", down)
    valid = jnp.repeat((neighbours[0] >= 0).astype(F32).T, 16, axis=1)
    turned = w_conv.transpose(0, 1, 2, 4, 3).reshape(3, 9, 64, 64)
    none = jnp.zeros_like(turned[0])
    w4 = jnp.stack(
        [
            jnp.concatenate([turned[0], turned[1]], axis=-1),
            jnp.concatenate([turned[2], none], axis=-1),
            jnp.concatenate([none, turned[0]], axis=-1),
            jnp.concatenate([turned[1], turned[2]], axis=-1),
        ],
        axis=1,
    )
    wd = w_down.transpose(1, 2, 0, 3, 4).reshape(512, 128)
    shape = jax.ShapeDtypeStruct
    saved = call(
        forward_kernel,
        (
            shape((4, 640, 512), BF16),
            shape((512, 512), F32),
            shape((512, 512), BF16),
            shape((128, 512), BF16),
            shape((128, 512), F32),
            shape((512, 256), F32),
        ),
        (feat, occupancy[0], valid, before, after, w4, wd, w_point),
        scratch=[pltpu.VMEM((640, 512), F32), pltpu.VMEM((256, 3456), BF16)],
        flops=4 * 10**9,
    )
    wire = call(
        backward_kernel,
        shape((2, HALF, LANES), BF16),
        (target, core, *saved, fetched, wd, w_point),
        scratch=[pltpu.VMEM((256, 1024), BF16)],
        flops=4 * 10**9,
        specs=[SMEM, SMEM] + [VMEM] * 9,
    )
    total = wire[0] + swap(wire[1], "brick", 1)
    halves = [total[: HALF // 2], total[HALF // 2 :]]
    bits = powers(dp_size, 1)
    for n in range(len(bits)):
        moved = [swap(part, "dp", bits[(n + s) % len(bits)]) for s, part in enumerate(halves)]
        halves = [a + b for a, b in zip(halves, moved)]
    total = jnp.concatenate(halves, axis=0)
    for bit in powers(brick_size, 2):
        total = total + swap(total, "brick", bit)
    other = swap(total, "brick", 1)
    gwc, gwd, gwp = call(
        finish_kernel,
        (shape((27, 64, 64), F32), shape((8, 64, 128), F32), shape((128, 256), F32)),
        (core, total, other),
        scratch=[pltpu.VMEM((2, HALF, LANES), BF16)],
        specs=[SMEM, VMEM, VMEM],
    )
    return gwc.reshape(3, 3, 3, 64, 64), gwd.reshape(2, 2, 2, 64, 128), gwp


def solution(mesh):
    in_specs = (
        P("dp", "brick", None, None),
        P("dp", "brick", None),
        P("dp", "brick", None),
        P("dp", "brick"),
        P(),
        P(),
        P(),
        P("dp", "brick", None, None),
    )
    out_specs = (P(), P(), P())
    return jax.shard_map(shards, mesh=mesh, in_specs=in_specs, out_specs=out_specs, check_vma=False)
```

```python
import functools

import jax
import jax.numpy as jnp
from jax import lax
from jax.experimental import pallas as pl
from jax.experimental.pallas import tpu as pltpu
from jax.sharding import PartitionSpec as P

F32 = jnp.float32
BF16 = jnp.bfloat16
LANES = 128
VMEM = pl.BlockSpec(memory_space=pltpu.VMEM)
HBM = pl.BlockSpec(memory_space=pltpu.HBM)
SMEM = pl.BlockSpec(memory_space=pltpu.SMEM)
COARSE_HALF, CONV_HALF = 384, 448


def mm(a, b, ca=1, cb=0):
    return lax.dot_general(a, b, (((ca,), (cb,)), ((), ())), preferred_element_type=F32)


def sigmoid(v):
    return 1.0 / (1.0 + jnp.exp(-v))


def turned_weights(w_conv):
    near = lax.broadcasted_iota(jnp.int32, (64, 64), 0) == lax.broadcasted_iota(jnp.int32, (64, 64), 1)
    eye = jnp.where(near, 1.0, 0.0).astype(BF16)
    zero = jnp.zeros((64, 64), BF16)
    first = jnp.concatenate([w_conv[9 * a + n] if a < 3 else zero for n in range(9) for a in range(4)], axis=0)
    second = jnp.concatenate([w_conv[9 * a + n] if a >= 0 else zero for n in range(9) for a in range(-1, 3)], axis=0)
    return mm(eye, first, 1, 1).astype(BF16), mm(eye, second, 1, 1).astype(BF16)


def near_masks(neighbours):
    brick = lax.broadcasted_iota(jnp.int32, (8, 128), 0)
    lane = lax.broadcasted_iota(jnp.int32, (8, 128), 1)
    spread = jnp.where(lane // 16 == brick, 1.0, 0.0)
    return mm(jnp.where(neighbours >= 0, 1.0, 0.0), spread, 0, 0)


def shift_planes(planes, valid, shifted):
    cell = lax.broadcasted_iota(jnp.int32, (1, 128), 1)
    q_at, r_at = cell // 4 % 4, cell % 4
    source = ((1, -1), (0, 0), (1, 0), (0, 1))
    for t in range(4):
        j, dq = source[t]
        for u in range(4):
            k, dr = source[u]
            g = 2 * j + k
            block = planes[:, 128 * g : 128 * g + 128]
            shift = -(4 * dq + dr) % 128
            if shift:
                block = pltpu.roll(block, shift, 1)
            if dr:
                inside = jnp.where((r_at + dr < 0) | (r_at + dr > 3), 0.0, 1.0)
            else:
                inside = jnp.ones((1, 128), F32)
            cross = None if dq == 0 else (q_at == 0 if dq < 0 else q_at == 3)
            for a, (lo, hi) in enumerate(((0, 64), (64, 576), (576, 640))):
                keep = inside
                near = valid[9 * a + 4 : 9 * a + 5]
                if cross is not None:
                    col = 9 * a + 3 * (dq + 1) + 1
                    keep = keep * jnp.where(cross, valid[col : col + 1], near)
                elif a != 1:
                    keep = keep * near
                part = block[lo:hi]
                if a != 1 or dq or dr:
                    part = part * keep.astype(part.dtype)
                shifted[t, lo:hi, 128 * u : 128 * u + 128] = part.astype(BF16)


def prepare_kernel(
    place, feat_hbm, occ_hbm, neighbours_hbm, w_conv_hbm, wd_hbm, wp_hbm, own_hbm,
    planes, occ_x, valid, wide, wd_rows, wp, own, beside, across,
    feat, occ, neighbours, w_conv, sems,
):
    copies = []
    for n, (source, target) in enumerate(
        ((feat_hbm, feat), (occ_hbm, occ), (w_conv_hbm, w_conv), (neighbours_hbm, neighbours), (wp_hbm, wp), (own_hbm, own))
    ):
        copies.append(pltpu.make_async_copy(source, target, sems.at[n]))
    for jk in range(4):
        for i in range(2):
            n = 2 * jk + i
            target = wd_rows.at[64 * n : 64 * n + 64]
            copies.append(pltpu.make_async_copy(wd_hbm.at[4 * i + jk], target, sems.at[6 + n]))
    for copy in copies:
        copy.start()
    lane = lax.broadcasted_iota(jnp.int32, (1, 512), 1)
    jj, kk, bb, qq, rr = lane // 256, lane // 128 % 2, lane % 128 // 16, lane // 4 % 4, lane % 4
    voxel = bb * 128 + 8 * (2 * qq + jj) + 2 * rr + kk
    row = lax.broadcasted_iota(jnp.int32, (1024, 512), 0)
    copies[0].wait()
    copies[1].wait()
    occ_f = occ[...].astype(F32).astype(BF16)
    rows = []
    for m in range(4):
        rows.append(jnp.concatenate([feat[b, :, 128 * m : 128 * m + 128] for b in range(8)], axis=1))
    occ_rows = [
        jnp.concatenate([occ_f[b : b + 1, 128 * m : 128 * m + 128] for b in range(8)], axis=1)
        for m in range(4)
    ]
    occ_rows = jnp.concatenate(occ_rows + [jnp.zeros((12, 1024), BF16)], axis=0)
    stacked = jnp.concatenate(rows + [occ_rows], axis=0)
    ends = []
    for e in range(2):
        select = jnp.where(row == voxel + 64 * e, 1.0, 0.0).astype(BF16)
        picked = mm(stacked, select)
        moved = picked[:256].astype(BF16)
        for m in range(4):
            planes[64 * (2 * m + e) : 64 * (2 * m + e + 1), :] = moved[64 * m : 64 * m + 64]
            occ_x[2 * m + e : 2 * m + e + 1] = picked[256 + m : 257 + m]
        ends.append(moved[192 * e : 192 * e + 64])
    even = place[0] == 0
    beside[...] = jnp.where(even, ends[1], ends[0])
    across[...] = jnp.where(even, ends[0], ends[1])
    copies[2].wait()
    first, second = turned_weights(w_conv)
    zero = jnp.zeros((64, 128), BF16)
    for n in range(9):
        cut = slice(256 * n, 256 * n + 256)
        for x in range(4):
            band = (first if x % 2 == 0 else second)[:, cut]
            band = [band, zero] if x < 2 else [zero, band]
            wide[64 * x : 64 * x + 64, 384 * n : 384 * n + 384] = jnp.concatenate(band, axis=1)
    copies[3].wait()
    valid[...] = near_masks(neighbours[...])
    for copy in copies[4:]:
        copy.wait()


def forward_kernel(
    place, inner, occ_x, valid, beside, across, wide, wd, wp,
    shifted, slope_pre, hid, coarse_ref, slope_down, slope_point,
    planes,
):
    planes[64:576] = inner[...]
    odd_core = place[0] == 1
    inner_x = lax.broadcasted_iota(jnp.int32, (64, 128), 1) >= 64
    for g in range(4):
        cut = slice(128 * g, 128 * g + 128)
        before = jnp.where(odd_core, beside[:, cut], across[:, cut])
        after = jnp.where(odd_core, across[:, cut], beside[:, cut])
        planes[0:64, cut] = pltpu.roll(jnp.where(inner_x, before, inner[448:512, cut]), 64, 1)
        planes[576:640, cut] = pltpu.roll(jnp.where(inner_x, inner[0:64, cut], after), 64, 1)
    shift_planes(planes, valid, shifted)
    for h in range(2):
        for j in range(2):
            taps = [
                shifted[j + b, 256 * h : 256 * h + 384, 128 * c : 128 * c + 256]
                for b in range(3)
                for c in range(3)
            ]
            pre = mm(wide[...], jnp.concatenate(taps, axis=0))
            gate = sigmoid(pre)
            for x in range(4):
                sub = slice(64 * x, 64 * x + 64)
                filled = occ_x[4 * h + x : 4 * h + x + 1, 256 * j : 256 * j + 256]
                act, g = pre[sub], gate[sub]
                r0 = 256 * h + 64 * x
                slope_pre[r0 : r0 + 64, 256 * j : 256 * j + 256] = filled * (g * (1.0 + act * (1.0 - g)))
                out = (act * g * filled).astype(BF16)
                p, i = 2 * h + x // 2, x % 2
                for k in range(2):
                    base = 128 * (2 * j + k) + 64 * i
                    hid[base : base + 64, 128 * p : 128 * p + 128] = out[:, 128 * k : 128 * k + 128]
    down = mm(wd[...], hid[...], 0, 0)
    gate = sigmoid(down)
    coarse = (down * gate).astype(BF16)
    coarse_ref[...] = coarse
    slope_down[...] = gate * (1.0 + down * (1.0 - gate))
    point = mm(coarse, wp[...], 0, 0)
    gate = sigmoid(point)
    slope_point[...] = gate * (1.0 + point * (1.0 - gate))


def pick_kernel(place, far_owners, own, beside, across, diagonal, near, reply):
    me = place[3]
    owners = [place[4 + b] for b in range(8)]
    tables = (own, beside, across, diagonal)

    def pick(relation, slot):
        value = own[slot]
        for n in range(1, 4):
            value = jnp.where(relation == n, tables[n][slot], value)
        return value

    for b in range(8):
        near[b] = pick(((owners[b] >> 3) ^ me) & 3, owners[b] & 7)
    for i in range(4):
        slot = jnp.int32(0)
        for b in range(8):
            slot = jnp.where((far_owners[b] >> 3) == (me & 4) + i, far_owners[b] & 7, slot)
        reply[i] = pick((me & 3) ^ i, slot)


def backward_kernel(
    split, place, shifted, slope_pre, hid, coarse, slope_down, slope_point, near, far, wd, wp, wire, wire_conv,
    grads,
):
    def put(target, first, value):
        half, at = divmod(first, target.shape[1])
        side = place[0] if half == 0 else 1 - place[0]
        target[side, at : at + value.shape[0]] = value.astype(BF16)

    parts = []
    for p in range(4):
        for b in range(8):
            part = near[b, 16 * p : 16 * p + 16, :]
            if split:
                target = place[4 + b] >> 3
                other = far[target & 3, 16 * p : 16 * p + 16, :]
                part = jnp.where(((target ^ place[3]) & 4) == 0, part, other)
            parts.append(part)
    cot_rows = jnp.concatenate(parts, axis=0)
    grad_point = (cot_rows.astype(F32) * slope_point[...]).astype(BF16)
    gwp = mm(coarse[...], grad_point)
    put(wire, 512, gwp[:, :128])
    put(wire, 640, gwp[:, 128:])
    grad_coarse = mm(wp[...], grad_point, 1, 1).astype(BF16)
    grad_down = (grad_coarse.astype(F32) * slope_down[...]).astype(BF16)
    gwd = mm(hid[...], grad_down, 1, 1)
    put(wire, 0, gwd[:384])
    put(wire, 384, gwd[384:])
    for jk in range(4):
        grad_hidden = mm(wd[128 * jk : 128 * jk + 128], grad_down)
        for p in range(4):
            cut = slice(128 * jk, 128 * jk + 128)
            value = grad_hidden[:, 128 * p : 128 * p + 128] * slope_pre[128 * p : 128 * p + 128, cut]
            h, base = p // 2, 128 * (p % 2)
            grads[base : base + 128, 512 * h + 128 * jk : 512 * h + 128 * jk + 128] = value.astype(BF16)
    low_lanes = lax.broadcasted_iota(jnp.int32, (64, 128), 1) < 64
    thirds = []
    for n in range(9):
        b, c = divmod(n, 3)
        left = jnp.concatenate(
            [
                shifted[j + b, 256 * h : 256 * h + 384, 128 * c : 128 * c + 256]
                for h in range(2)
                for j in range(2)
            ],
            axis=1,
        )
        band = mm(left, grads[...], 1, 1)
        sums = []
        for a in range(3):
            even = band[64 * a : 64 * a + 64, :128] + band[64 * a + 128 : 64 * a + 192, 128:]
            odd = band[64 * a + 64 : 64 * a + 128, :128] + band[64 * a + 192 : 64 * a + 256, 128:]
            both = jnp.where(low_lanes, even, odd)
            sums.append(both + pltpu.roll(both, 64, 1))
        put(wire_conv, 64 * n, jnp.where(low_lanes, sums[0], sums[1]))
        thirds.append(sums[2])
    for n in range(5):
        put(wire_conv, 64 * (9 + n), jnp.where(low_lanes, thirds[2 * n], thirds[min(2 * n + 1, 8)]))


def rows_of(place, mine, other, first, count):
    half, at = divmod(first, mine.shape[0])
    return jnp.where(place[0] == half, mine[at : at + count], other[at : at + count]).astype(F32)


def finish_coarse_kernel(place, mine, other, gwd, gwp):
    for i in range(2):
        for jk in range(4):
            gwd[4 * i + jk] = rows_of(place, mine, other, 128 * jk + 64 * i, 64)
    for s in range(2):
        gwp[:, 128 * s : 128 * s + 128] = rows_of(place, mine, other, 512 + 128 * s, 128)


def finish_conv_kernel(place, mine, other, gwc):
    for n in range(9):
        pair = rows_of(place, mine, other, 64 * n, 64)
        gwc[n] = pair[:, :64]
        gwc[9 + n] = pair[:, 64:]
    for n in range(5):
        pair = rows_of(place, mine, other, 64 * (9 + n), 64)
        gwc[18 + 2 * n] = pair[:, :64]
        if n < 4:
            gwc[19 + 2 * n] = pair[:, 64:]


def call(kernel, outs, ins, scratch=(), limit=24 * 2**20, flops=0, specs=None):
    return pl.pallas_call(
        kernel,
        out_shape=outs,
        in_specs=specs or [VMEM] * len(ins),
        out_specs=jax.tree.map(lambda _: VMEM, outs),
        scratch_shapes=scratch,
        compiler_params=pltpu.CompilerParams(vmem_limit_bytes=limit),
        cost_estimate=pl.CostEstimate(flops=flops, bytes_accessed=2**20, transcendentals=0),
    )(*ins)


def in_hbm(*arrays):
    return [pltpu.with_memory_space_constraint(array, pltpu.HBM) for array in arrays]


def swap(value, axis, bit):
    size = lax.axis_size(axis)
    return lax.ppermute(value, axis, [(i, i ^ bit) for i in range(size)])


def powers(size, first):
    bits = []
    while first < size:
        bits.append(first)
        first *= 2
    return bits


def shards(features, occupancy, neighbours, owners, w_conv, w_down, w_point, cotangent):
    brick_size = lax.axis_size("brick")
    shape = jax.ShapeDtypeStruct
    me = lax.axis_index("brick")
    core = me & 1
    dp_at = lax.axis_index("dp")
    feat = jnp.swapaxes(features[0], 1, 2)
    slots, own = owners[0], cotangent[0]
    split = brick_size == 8
    place = jnp.concatenate([jnp.stack([core, dp_at & 1, dp_at >> 1, me]).astype(jnp.int32), slots])
    prepared = call(
        prepare_kernel,
        (
            shape((512, 512), BF16),
            shape((8, 512), F32),
            shape((27, 128), F32),
            shape((256, 3456), BF16),
            shape((512, 128), BF16),
            shape((128, 256), BF16),
            shape((8, 64, 256), BF16),
            shape((64, 512), BF16),
            shape((64, 512), BF16),
        ),
        (place, *in_hbm(feat, occupancy[0], neighbours[0], w_conv.reshape(27, 64, 64), w_down.reshape(8, 64, 128), w_point, own)),
        scratch=[
            pltpu.VMEM((8, 64, 512), BF16),
            pltpu.VMEM((8, 512), jnp.int32),
            pltpu.VMEM((8, 27), jnp.int32),
            pltpu.VMEM((27, 64, 64), BF16),
            pltpu.SemaphoreType.DMA((14,)),
        ],
        flops=4 * 10**9,
        specs=[SMEM] + [HBM] * 7,
    )
    planes, occ_x, valid, wide, wd, wp, own_copy, beside, across = prepared
    beside = swap(beside, "brick", 1)
    chips = [(i, i + 1) for i in range(1, brick_size - 1, 2)]
    across = lax.ppermute(across, "brick", chips + [(j, i) for i, j in chips])
    if split:
        partner, far_slots, planes = lax.optimization_barrier((swap(own, "brick", 2), swap(slots, "brick", 4), planes))
        tables = (own_copy, swap(own, "brick", 1), partner, swap(partner, "brick", 1))
        near, reply = call(
            pick_kernel,
            (shape((8, 64, 256), BF16), shape((4, 64, 256), BF16)),
            (place, far_slots, *tables),
            specs=[SMEM] * 2 + [VMEM] * 4,
        )
        far = swap(reply, "brick", 4)
    else:
        wanted = jnp.arange(brick_size, dtype=jnp.int32)[:, None] == (slots >> 3)[None, :]
        request = jnp.max(jnp.where(wanted, (slots & 7)[None, :], 0), axis=1)
        arrived = lax.all_to_all(request, "brick", split_axis=0, concat_axis=0, tiled=True)
        reply = jnp.take(own, arrived, axis=0, mode="clip")
        fetched = lax.all_to_all(reply, "brick", split_axis=0, concat_axis=0, tiled=True)
        near = jnp.take(fetched, slots >> 3, axis=0, mode="clip")
        far = near[:4]
    saved = call(
        forward_kernel,
        (
            shape((4, 640, 512), BF16),
            shape((512, 512), F32),
            shape((512, 512), BF16),
            shape((128, 512), BF16),
            shape((128, 512), F32),
            shape((512, 256), F32),
        ),
        (place, planes, occ_x, valid, beside, across, wide, wd, wp),
        scratch=[pltpu.VMEM((640, 512), BF16)],
        flops=4 * 10**9,
        specs=[SMEM] + [VMEM] * 8,
    )
    wires = call(
        functools.partial(backward_kernel, split),
        (shape((2, COARSE_HALF, 128), BF16), shape((2, CONV_HALF, 128), BF16)),
        (place, *saved, near, far, wd, wp),
        scratch=[pltpu.VMEM((256, 1024), BF16)],
        flops=4 * 10**9,
        specs=[SMEM] + [VMEM] * 10,
    )
    bits = powers(brick_size, 4)[::-1]
    far_steps = [("brick", bit) for bit in bits]
    orders = (far_steps + [("dp", 1), ("brick", 2), ("dp", 2)], [("dp", 1)] + far_steps + [("dp", 2), ("brick", 2)])
    sums = [wire[0] + swap(wire[1], "brick", 1) for wire in wires]
    for n in range(len(orders[0])):
        for s in range(2):
            sums[s] = sums[s] + swap(sums[s], *orders[s][n])
    others = [swap(total, "brick", 1) for total in sums]
    specs = [SMEM, VMEM, VMEM]
    gwd, gwp = call(
        finish_coarse_kernel,
        (shape((8, 64, 128), F32), shape((128, 256), F32)),
        (place, sums[0], others[0]),
        specs=specs,
    )
    gwc = call(finish_conv_kernel, shape((27, 64, 64), F32), (place, sums[1], others[1]), specs=specs)
    return gwc.reshape(3, 3, 3, 64, 64), gwd.reshape(2, 2, 2, 64, 128), gwp


def solution(mesh):
    in_specs = (
        P("dp", "brick", None, None),
        P("dp", "brick", None),
        P("dp", "brick", None),
        P("dp", "brick"),
        P(),
        P(),
        P(),
        P("dp", "brick", None, None),
    )
    out_specs = (P(), P(), P())
    return jax.shard_map(shards, mesh=mesh, in_specs=in_specs, out_specs=out_specs, check_vma=False)
```

```python
import functools

import jax
import jax.numpy as jnp
from jax import lax
from jax.experimental import pallas as pl
from jax.experimental.pallas import tpu as pltpu
from jax.sharding import PartitionSpec as P

F32 = jnp.float32
BF16 = jnp.bfloat16
LANES = 128
VMEM = pl.BlockSpec(memory_space=pltpu.VMEM)
HBM = pl.BlockSpec(memory_space=pltpu.HBM)
SMEM = pl.BlockSpec(memory_space=pltpu.SMEM)
POINT_AT, CONV_AT = 512, 768
PART = 416


def mm(a, b, ca=1, cb=0):
    return lax.dot_general(a, b, (((ca,), (cb,)), ((), ())), preferred_element_type=F32)


def sigmoid(v):
    return 1.0 / (1.0 + jnp.exp(-v))


def turned_weights(w_conv):
    near = lax.broadcasted_iota(jnp.int32, (64, 64), 0) == lax.broadcasted_iota(jnp.int32, (64, 64), 1)
    eye = jnp.where(near, 1.0, 0.0).astype(BF16)
    zero = jnp.zeros((64, 64), BF16)
    first = jnp.concatenate([w_conv[9 * a + n] if a < 3 else zero for n in range(9) for a in range(4)], axis=0)
    second = jnp.concatenate([w_conv[9 * a + n] if a >= 0 else zero for n in range(9) for a in range(-1, 3)], axis=0)
    return mm(eye, first, 1, 1).astype(BF16), mm(eye, second, 1, 1).astype(BF16)


def near_masks(neighbours):
    brick = lax.broadcasted_iota(jnp.int32, (8, 128), 0)
    lane = lax.broadcasted_iota(jnp.int32, (8, 128), 1)
    spread = jnp.where(lane // 16 == brick, 1.0, 0.0)
    return mm(jnp.where(neighbours >= 0, 1.0, 0.0), spread, 0, 0)


def shift_planes(planes, valid, shifted):
    cell = lax.broadcasted_iota(jnp.int32, (1, 128), 1)
    q_at, r_at = cell // 4 % 4, cell % 4
    source = ((1, -1), (0, 0), (1, 0), (0, 1))
    for t in range(4):
        j, dq = source[t]
        for u in range(4):
            k, dr = source[u]
            g = 2 * j + k
            block = planes[:, 128 * g : 128 * g + 128]
            shift = -(4 * dq + dr) % 128
            if shift:
                block = pltpu.roll(block, shift, 1)
            if dr:
                inside = jnp.where((r_at + dr < 0) | (r_at + dr > 3), 0.0, 1.0)
            else:
                inside = jnp.ones((1, 128), F32)
            cross = None if dq == 0 else (q_at == 0 if dq < 0 else q_at == 3)
            for a, (lo, hi) in enumerate(((0, 64), (64, 576), (576, 640))):
                keep = inside
                near = valid[9 * a + 4 : 9 * a + 5]
                if cross is not None:
                    col = 9 * a + 3 * (dq + 1) + 1
                    keep = keep * jnp.where(cross, valid[col : col + 1], near)
                elif a != 1:
                    keep = keep * near
                part = block[lo:hi]
                if a != 1 or dq or dr:
                    part = part * keep.astype(part.dtype)
                shifted[t, lo:hi, 128 * u : 128 * u + 128] = part.astype(BF16)


def voxel_at():
    lane = lax.broadcasted_iota(jnp.int32, (1, 512), 1)
    jj, kk, bb, qq, rr = lane // 256, lane // 128 % 2, lane % 128 // 16, lane // 4 % 4, lane % 4
    return bb * 128 + 8 * (2 * qq + jj) + 2 * rr + kk


def prepare_kernel(
    place, feat_hbm, occ_hbm, neighbours_hbm, w_conv_hbm, wd_hbm, wp_hbm, own_hbm,
    planes, occ_x, valid, wide, wd_rows, wp, own, beside, across,
    feat, occ, neighbours, w_conv, sems,
):
    copies = []
    for n, (source, target) in enumerate(
        ((feat_hbm, feat), (occ_hbm, occ), (w_conv_hbm, w_conv), (neighbours_hbm, neighbours), (wp_hbm, wp), (own_hbm, own))
    ):
        copies.append(pltpu.make_async_copy(source, target, sems.at[n]))
    for jk in range(4):
        for i in range(2):
            n = 2 * jk + i
            target = wd_rows.at[64 * n : 64 * n + 64]
            copies.append(pltpu.make_async_copy(wd_hbm.at[4 * i + jk], target, sems.at[6 + n]))
    for copy in copies:
        copy.start()
    voxel = voxel_at()
    row = lax.broadcasted_iota(jnp.int32, (1024, 512), 0)
    copies[0].wait()
    copies[1].wait()
    occ_f = occ[...].astype(F32).astype(BF16)
    rows = []
    for m in range(4):
        rows.append(jnp.concatenate([feat[b, :, 128 * m : 128 * m + 128] for b in range(8)], axis=1))
    occ_rows = [
        jnp.concatenate([occ_f[b : b + 1, 128 * m : 128 * m + 128] for b in range(8)], axis=1)
        for m in range(4)
    ]
    occ_rows = jnp.concatenate(occ_rows + [jnp.zeros((12, 1024), BF16)], axis=0)
    stacked = jnp.concatenate(rows + [occ_rows], axis=0)
    ends = []
    for e in range(2):
        select = jnp.where(row == voxel + 64 * e, 1.0, 0.0).astype(BF16)
        picked = mm(stacked, select)
        moved = picked[:256].astype(BF16)
        for m in range(4):
            planes[64 * (2 * m + e) : 64 * (2 * m + e + 1), :] = moved[64 * m : 64 * m + 64]
            occ_x[2 * m + e : 2 * m + e + 1] = picked[256 + m : 257 + m]
        ends.append(moved[192 * e : 192 * e + 64])
    even = place[0] == 0
    beside[...] = jnp.where(even, ends[1], ends[0])
    across[...] = jnp.where(even, ends[0], ends[1])
    copies[2].wait()
    first, second = turned_weights(w_conv)
    zero = jnp.zeros((64, 128), BF16)
    for n in range(9):
        cut = slice(256 * n, 256 * n + 256)
        for x in range(4):
            band = (first if x % 2 == 0 else second)[:, cut]
            band = [band, zero] if x < 2 else [zero, band]
            wide[64 * x : 64 * x + 64, 384 * n : 384 * n + 384] = jnp.concatenate(band, axis=1)
    copies[3].wait()
    valid[...] = near_masks(neighbours[...])
    for copy in copies[4:]:
        copy.wait()


def forward_kernel(
    place, inner, occ_x, valid, beside, across, wide, wd, wp,
    shifted, slope_pre, hid, coarse_ref, slope_down, slope_point,
    planes,
):
    planes[64:576] = inner[...]
    odd_core = place[0] == 1
    inner_x = lax.broadcasted_iota(jnp.int32, (64, 128), 1) >= 64
    for g in range(4):
        cut = slice(128 * g, 128 * g + 128)
        before = jnp.where(odd_core, beside[:, cut], across[:, cut])
        after = jnp.where(odd_core, across[:, cut], beside[:, cut])
        planes[0:64, cut] = pltpu.roll(jnp.where(inner_x, before, inner[448:512, cut]), 64, 1)
        planes[576:640, cut] = pltpu.roll(jnp.where(inner_x, inner[0:64, cut], after), 64, 1)
    shift_planes(planes, valid, shifted)
    for h in range(2):
        for j in range(2):
            taps = [
                shifted[j + b, 256 * h : 256 * h + 384, 128 * c : 128 * c + 256]
                for b in range(3)
                for c in range(3)
            ]
            pre = mm(wide[...], jnp.concatenate(taps, axis=0))
            gate = sigmoid(pre)
            for x in range(4):
                sub = slice(64 * x, 64 * x + 64)
                filled = occ_x[4 * h + x : 4 * h + x + 1, 256 * j : 256 * j + 256]
                act, g = pre[sub], gate[sub]
                r0 = 256 * h + 64 * x
                slope_pre[r0 : r0 + 64, 256 * j : 256 * j + 256] = filled * (g * (1.0 + act * (1.0 - g)))
                out = (act * g * filled).astype(BF16)
                p, i = 2 * h + x // 2, x % 2
                for k in range(2):
                    base = 128 * (2 * j + k) + 64 * i
                    hid[base : base + 64, 128 * p : 128 * p + 128] = out[:, 128 * k : 128 * k + 128]
    down = mm(wd[...], hid[...], 0, 0)
    gate = sigmoid(down)
    coarse = (down * gate).astype(BF16)
    coarse_ref[...] = coarse
    slope_down[...] = gate * (1.0 + down * (1.0 - gate))
    point = mm(coarse, wp[...], 0, 0)
    gate = sigmoid(point)
    slope_point[...] = gate * (1.0 + point * (1.0 - gate))


def pick_kernel(place, far_owners, own, beside, across, diagonal, near, reply):
    me = place[3]
    owners = [place[4 + b] for b in range(8)]
    tables = (own, beside, across, diagonal)

    def pick(relation, slot):
        value = own[slot]
        for n in range(1, 4):
            value = jnp.where(relation == n, tables[n][slot], value)
        return value

    for b in range(8):
        near[b] = pick(((owners[b] >> 3) ^ me) & 3, owners[b] & 7)
    for i in range(4):
        slot = jnp.int32(0)
        for b in range(8):
            slot = jnp.where((far_owners[b] >> 3) == (me & 4) + i, far_owners[b] & 7, slot)
        reply[i] = pick((me & 3) ^ i, slot)


def backward_kernel(
    split, place, shifted, slope_pre, hid, coarse, slope_down, slope_point, near, far, wd, wp, wire,
    grads,
):
    def put(first, value):
        done = 0
        while done < value.shape[0]:
            (stream, half), at = divmod((first + done) // PART, 2), (first + done) % PART
            size = min(value.shape[0] - done, PART - at)
            side = place[0] if half == 0 else 1 - place[0]
            wire[side, stream, at : at + size] = value[done : done + size].astype(BF16)
            done += size

    parts = []
    for p in range(4):
        for b in range(8):
            part = near[b, 16 * p : 16 * p + 16, :]
            if split:
                target = place[4 + b] >> 3
                other = far[target & 3, 16 * p : 16 * p + 16, :]
                part = jnp.where(((target ^ place[3]) & 4) == 0, part, other)
            parts.append(part)
    cot_rows = jnp.concatenate(parts, axis=0)
    grad_point = (cot_rows.astype(F32) * slope_point[...]).astype(BF16)
    gwp = mm(coarse[...], grad_point)
    put(POINT_AT, gwp[:, :128])
    put(POINT_AT + 128, gwp[:, 128:])
    grad_coarse = mm(wp[...], grad_point, 1, 1).astype(BF16)
    grad_down = (grad_coarse.astype(F32) * slope_down[...]).astype(BF16)
    put(0, mm(hid[...], grad_down, 1, 1))
    for jk in range(4):
        grad_hidden = mm(wd[128 * jk : 128 * jk + 128], grad_down)
        for p in range(4):
            cut = slice(128 * jk, 128 * jk + 128)
            value = grad_hidden[:, 128 * p : 128 * p + 128] * slope_pre[128 * p : 128 * p + 128, cut]
            h, base = p // 2, 128 * (p % 2)
            grads[base : base + 128, 512 * h + 128 * jk : 512 * h + 128 * jk + 128] = value.astype(BF16)
    low_lanes = lax.broadcasted_iota(jnp.int32, (64, 128), 1) < 64
    thirds = []
    for n in range(9):
        b, c = divmod(n, 3)
        left = jnp.concatenate(
            [
                shifted[j + b, 256 * h : 256 * h + 384, 128 * c : 128 * c + 256]
                for h in range(2)
                for j in range(2)
            ],
            axis=1,
        )
        band = mm(left, grads[...], 1, 1)
        sums = []
        for a in range(3):
            even = band[64 * a : 64 * a + 64, :128] + band[64 * a + 128 : 64 * a + 192, 128:]
            odd = band[64 * a + 64 : 64 * a + 128, :128] + band[64 * a + 192 : 64 * a + 256, 128:]
            both = jnp.where(low_lanes, even, odd)
            sums.append(both + pltpu.roll(both, 64, 1))
        put(CONV_AT + 64 * n, jnp.where(low_lanes, sums[0], sums[1]))
        thirds.append(sums[2])
    for n in range(5):
        put(CONV_AT + 64 * (9 + n), jnp.where(low_lanes, thirds[2 * n], thirds[min(2 * n + 1, 8)]))


def finish_kernel(mine_a, other_a, mine_b, other_b, gwc, gwd, gwp):
    def emit(halves):
        def rows(first, count):
            parts = []
            while count:
                (stream, half), at = divmod(first // PART, 2), first % PART
                size = min(count, PART - at)
                parts.append(halves[half][stream][at : at + size].astype(F32))
                first, count = first + size, count - size
            return jnp.concatenate(parts, axis=0) if len(parts) > 1 else parts[0]

        for i in range(2):
            for jk in range(4):
                gwd[4 * i + jk] = rows(128 * jk + 64 * i, 64)
        for n in range(2):
            gwp[:, 128 * n : 128 * n + 128] = rows(POINT_AT + 128 * n, 128)
        for n in range(14):
            pair = rows(CONV_AT + 64 * n, 64)
            first, second = (n, 9 + n) if n < 9 else (2 * n, 2 * n + 1)
            gwc[first] = pair[:, :64]
            if second < 27:
                gwc[second] = pair[:, 64:]

    core = lax.axis_index("brick") & 1
    mine, other = (mine_a, mine_b), (other_a, other_b)
    pl.when(core == 0)(lambda: emit((mine, other)))
    pl.when(core == 1)(lambda: emit((other, mine)))


def call(kernel, outs, ins, scratch=(), limit=24 * 2**20, flops=0, specs=None):
    return pl.pallas_call(
        kernel,
        out_shape=outs,
        in_specs=specs or [VMEM] * len(ins),
        out_specs=jax.tree.map(lambda _: VMEM, outs),
        scratch_shapes=scratch,
        compiler_params=pltpu.CompilerParams(vmem_limit_bytes=limit),
        cost_estimate=pl.CostEstimate(flops=flops, bytes_accessed=2**20, transcendentals=0),
    )(*ins)


def in_hbm(*arrays):
    return [pltpu.with_memory_space_constraint(array, pltpu.HBM) for array in arrays]


def swap(value, axis, bit):
    size = lax.axis_size(axis)
    return lax.ppermute(value, axis, [(i, i ^ bit) for i in range(size)])


def powers(size, first):
    bits = []
    while first < size:
        bits.append(first)
        first *= 2
    return bits


def shards(features, occupancy, neighbours, owners, w_conv, w_down, w_point, cotangent):
    brick_size = lax.axis_size("brick")
    shape = jax.ShapeDtypeStruct
    me = lax.axis_index("brick")
    core = me & 1
    dp_at = lax.axis_index("dp")
    feat = jnp.swapaxes(features[0], 1, 2)
    slots, own = owners[0], cotangent[0]
    split = brick_size == 8
    place = jnp.concatenate([jnp.stack([core, dp_at & 1, dp_at >> 1, me]).astype(jnp.int32), slots])
    prepared = call(
        prepare_kernel,
        (
            shape((512, 512), BF16),
            shape((8, 512), F32),
            shape((27, 128), F32),
            shape((256, 3456), BF16),
            shape((512, 128), BF16),
            shape((128, 256), BF16),
            shape((8, 64, 256), BF16),
            shape((64, 512), BF16),
            shape((64, 512), BF16),
        ),
        (place, *in_hbm(feat, occupancy[0], neighbours[0], w_conv.reshape(27, 64, 64), w_down.reshape(8, 64, 128), w_point, own)),
        scratch=[
            pltpu.VMEM((8, 64, 512), BF16),
            pltpu.VMEM((8, 512), jnp.int32),
            pltpu.VMEM((8, 27), jnp.int32),
            pltpu.VMEM((27, 64, 64), BF16),
            pltpu.SemaphoreType.DMA((14,)),
        ],
        flops=4 * 10**9,
        specs=[SMEM] + [HBM] * 7,
    )
    planes, occ_x, valid, wide, wd, wp, own_copy, beside, across = prepared
    beside = swap(beside, "brick", 1)
    chips = [(i, i + 1) for i in range(1, brick_size - 1, 2)]
    across = lax.ppermute(across, "brick", chips + [(j, i) for i, j in chips])
    if split:
        partner, far_slots, planes = lax.optimization_barrier((swap(own, "brick", 2), swap(slots, "brick", 4), planes))
        tables = (own_copy, swap(own, "brick", 1), partner, swap(partner, "brick", 1))
        near, reply = call(
            pick_kernel,
            (shape((8, 64, 256), BF16), shape((4, 64, 256), BF16)),
            (place, far_slots, *tables),
            specs=[SMEM] * 2 + [VMEM] * 4,
        )
        far = swap(reply, "brick", 4)
    else:
        wanted = jnp.arange(brick_size, dtype=jnp.int32)[:, None] == (slots >> 3)[None, :]
        request = jnp.max(jnp.where(wanted, (slots & 7)[None, :], 0), axis=1)
        arrived = lax.all_to_all(request, "brick", split_axis=0, concat_axis=0, tiled=True)
        reply = jnp.take(own, arrived, axis=0, mode="clip")
        fetched = lax.all_to_all(reply, "brick", split_axis=0, concat_axis=0, tiled=True)
        near = jnp.take(fetched, slots >> 3, axis=0, mode="clip")
        far = near[:4]
    saved = call(
        forward_kernel,
        (
            shape((4, 640, 512), BF16),
            shape((512, 512), F32),
            shape((512, 512), BF16),
            shape((128, 512), BF16),
            shape((128, 512), F32),
            shape((512, 256), F32),
        ),
        (place, planes, occ_x, valid, beside, across, wide, wd, wp),
        scratch=[pltpu.VMEM((640, 512), BF16)],
        flops=4 * 10**9,
        specs=[SMEM] + [VMEM] * 8,
    )
    wire = call(
        functools.partial(backward_kernel, split),
        shape((2, 2, PART, 128), BF16),
        (place, *saved, near, far, wd, wp),
        scratch=[pltpu.VMEM((256, 1024), BF16)],
        flops=4 * 10**9,
        specs=[SMEM] + [VMEM] * 10,
    )
    far_steps = [("brick", bit) for bit in powers(brick_size, 4)]
    x, y, z = [("dp", 1)], [("dp", 2)], [("brick", 2)]
    orders = z + x + y + far_steps, x + y + far_steps + z
    sums = [wire[0, n] + swap(wire[1, n], "brick", 1) for n in range(2)]
    for n in range(len(orders[0])):
        for stream in range(2):
            sums[stream] = sums[stream] + swap(sums[stream], *orders[stream][n])
    others = [swap(total, "brick", 1) for total in sums]
    gwc, gwd, gwp = call(
        finish_kernel,
        (shape((27, 64, 64), F32), shape((8, 64, 128), F32), shape((128, 256), F32)),
        (sums[0], others[0], sums[1], others[1]),
    )
    return gwc.reshape(3, 3, 3, 64, 64), gwd.reshape(2, 2, 2, 64, 128), gwp


def solution(mesh):
    in_specs = (
        P("dp", "brick", None, None),
        P("dp", "brick", None),
        P("dp", "brick", None),
        P("dp", "brick"),
        P(),
        P(),
        P(),
        P("dp", "brick", None, None),
    )
    out_specs = (P(), P(), P())
    return jax.shard_map(shards, mesh=mesh, in_specs=in_specs, out_specs=out_specs, check_vma=False)
```

```python
import jax
import jax.numpy as jnp
from jax import lax
from jax.experimental import pallas as pl
from jax.experimental.pallas import tpu as pltpu
from jax.sharding import PartitionSpec as P

F32 = jnp.float32
BF16 = jnp.bfloat16
LANES = 128
VMEM = pl.BlockSpec(memory_space=pltpu.VMEM)
HBM = pl.BlockSpec(memory_space=pltpu.HBM)
SMEM = pl.BlockSpec(memory_space=pltpu.SMEM)
POINT_AT, CONV_AT = 512, 768
PART = 416


def mm(a, b, ca=1, cb=0):
    return lax.dot_general(a, b, (((ca,), (cb,)), ((), ())), preferred_element_type=F32)


def sigmoid(v):
    return 1.0 / (1.0 + jnp.exp(-v))


def turned_weights(w_conv):
    near = lax.broadcasted_iota(jnp.int32, (64, 64), 0) == lax.broadcasted_iota(jnp.int32, (64, 64), 1)
    eye = jnp.where(near, 1.0, 0.0).astype(BF16)
    zero = jnp.zeros((64, 64), BF16)
    first = jnp.concatenate([w_conv[9 * a + n] if a < 3 else zero for n in range(9) for a in range(4)], axis=0)
    second = jnp.concatenate([w_conv[9 * a + n] if a >= 0 else zero for n in range(9) for a in range(-1, 3)], axis=0)
    return mm(eye, first, 1, 1).astype(BF16), mm(eye, second, 1, 1).astype(BF16)


def near_masks(neighbours):
    brick = lax.broadcasted_iota(jnp.int32, (8, 128), 0)
    lane = lax.broadcasted_iota(jnp.int32, (8, 128), 1)
    spread = jnp.where(lane // 16 == brick, 1.0, 0.0)
    return mm(jnp.where(neighbours >= 0, 1.0, 0.0), spread, 0, 0)


def shift_planes(planes, valid, shifted):
    cell = lax.broadcasted_iota(jnp.int32, (1, 128), 1)
    q_at, r_at = cell // 4 % 4, cell % 4
    source = ((1, -1), (0, 0), (1, 0), (0, 1))
    for t in range(4):
        j, dq = source[t]
        for u in range(4):
            k, dr = source[u]
            g = 2 * j + k
            block = planes[:, 128 * g : 128 * g + 128]
            shift = -(4 * dq + dr) % 128
            if shift:
                block = pltpu.roll(block, shift, 1)
            if dr:
                inside = jnp.where((r_at + dr < 0) | (r_at + dr > 3), 0.0, 1.0)
            else:
                inside = jnp.ones((1, 128), F32)
            cross = None if dq == 0 else (q_at == 0 if dq < 0 else q_at == 3)
            for a, (lo, hi) in enumerate(((0, 64), (64, 576), (576, 640))):
                keep = inside
                near = valid[9 * a + 4 : 9 * a + 5]
                if cross is not None:
                    col = 9 * a + 3 * (dq + 1) + 1
                    keep = keep * jnp.where(cross, valid[col : col + 1], near)
                elif a != 1:
                    keep = keep * near
                part = block[lo:hi]
                if a != 1 or dq or dr:
                    part = part * keep.astype(part.dtype)
                shifted[t, lo:hi, 128 * u : 128 * u + 128] = part.astype(BF16)


def voxel_at():
    lane = lax.broadcasted_iota(jnp.int32, (1, 512), 1)
    jj, kk, bb, qq, rr = lane // 256, lane // 128 % 2, lane % 128 // 16, lane // 4 % 4, lane % 4
    return bb * 128 + 8 * (2 * qq + jj) + 2 * rr + kk


def prepare_kernel(
    feat_hbm, occ_hbm, neighbours_hbm, w_conv_hbm, wd_hbm, wp_hbm, own_hbm, slots_hbm,
    planes, occ_x, valid, wide, wd_rows, wp, own, slots,
    feat, occ, neighbours, w_conv, sems,
):
    pairs = [(w_conv_hbm, w_conv), (feat_hbm, feat), (occ_hbm, occ), (neighbours_hbm, neighbours)]
    pairs += [(wp_hbm, wp), (own_hbm, own), (slots_hbm, slots)]
    for jk in range(4):
        for i in range(2):
            n = 2 * jk + i
            pairs.append((wd_hbm.at[4 * i + jk], wd_rows.at[64 * n : 64 * n + 64]))
    copies = [pltpu.make_async_copy(source, target, sems.at[n]) for n, (source, target) in enumerate(pairs)]
    for copy in copies:
        copy.start()
    copies[0].wait()
    first, second = turned_weights(w_conv)
    zero = jnp.zeros((64, 128), BF16)
    for n in range(9):
        cut = slice(256 * n, 256 * n + 256)
        for x in range(4):
            band = (first if x % 2 == 0 else second)[:, cut]
            band = [band, zero] if x < 2 else [zero, band]
            wide[64 * x : 64 * x + 64, 384 * n : 384 * n + 384] = jnp.concatenate(band, axis=1)
    voxel = voxel_at()
    row = lax.broadcasted_iota(jnp.int32, (1024, 512), 0)
    copies[1].wait()
    copies[2].wait()
    occ_f = occ[...].astype(F32).astype(BF16)
    rows = []
    for m in range(4):
        rows.append(jnp.concatenate([feat[b, :, 128 * m : 128 * m + 128] for b in range(8)], axis=1))
    occ_rows = [
        jnp.concatenate([occ_f[b : b + 1, 128 * m : 128 * m + 128] for b in range(8)], axis=1)
        for m in range(4)
    ]
    occ_rows = jnp.concatenate(occ_rows + [jnp.zeros((12, 1024), BF16)], axis=0)
    stacked = jnp.concatenate(rows + [occ_rows], axis=0)
    for e in range(2):
        select = jnp.where(row == voxel + 64 * e, 1.0, 0.0).astype(BF16)
        picked = mm(stacked, select)
        for m in range(4):
            planes[64 * (2 * m + e) : 64 * (2 * m + e + 1), :] = picked[64 * m : 64 * m + 64].astype(BF16)
            occ_x[2 * m + e : 2 * m + e + 1] = picked[256 + m : 257 + m]
    copies[3].wait()
    valid[...] = near_masks(neighbours[...])
    for copy in copies[4:]:
        copy.wait()


def forward_kernel(
    inner, occ_x, valid, beside, across, wide, wd, wp,
    shifted, slope_pre, hid, coarse_ref, slope_down, slope_point,
    planes,
):
    planes[64:576] = inner[...]
    odd_core = lax.axis_index("brick") & 1 == 1
    inner_x = lax.broadcasted_iota(jnp.int32, (64, 128), 1) >= 64
    row = lax.broadcasted_iota(jnp.int32, (512, 512), 0)
    before = jnp.concatenate([jnp.where(odd_core, beside[b], across[b]) for b in range(4)], axis=1)
    after = jnp.concatenate([jnp.where(odd_core, across[b], beside[b]) for b in range(4)], axis=1)
    before = mm(before, jnp.where(row == voxel_at() - 448, 1.0, 0.0).astype(BF16)).astype(BF16)
    after = mm(after, jnp.where(row == voxel_at(), 1.0, 0.0).astype(BF16)).astype(BF16)
    for g in range(4):
        cut = slice(128 * g, 128 * g + 128)
        planes[0:64, cut] = pltpu.roll(jnp.where(inner_x, before[:, cut], inner[448:512, cut]), 64, 1)
        planes[576:640, cut] = pltpu.roll(jnp.where(inner_x, inner[0:64, cut], after[:, cut]), 64, 1)
    shift_planes(planes, valid, shifted)
    for h in range(2):
        for j in range(2):
            taps = [
                shifted[j + b, 256 * h : 256 * h + 384, 128 * c : 128 * c + 256]
                for b in range(3)
                for c in range(3)
            ]
            pre = mm(wide[...], jnp.concatenate(taps, axis=0))
            gate = sigmoid(pre)
            for x in range(4):
                sub = slice(64 * x, 64 * x + 64)
                filled = occ_x[4 * h + x : 4 * h + x + 1, 256 * j : 256 * j + 256]
                act, g = pre[sub], gate[sub]
                r0 = 256 * h + 64 * x
                slope_pre[r0 : r0 + 64, 256 * j : 256 * j + 256] = filled * (g * (1.0 + act * (1.0 - g)))
                out = (act * g * filled).astype(BF16)
                p, i = 2 * h + x // 2, x % 2
                for k in range(2):
                    base = 128 * (2 * j + k) + 64 * i
                    hid[base : base + 64, 128 * p : 128 * p + 128] = out[:, 128 * k : 128 * k + 128]
    down = mm(wd[...], hid[...], 0, 0)
    gate = sigmoid(down)
    coarse = (down * gate).astype(BF16)
    coarse_ref[...] = coarse
    slope_down[...] = gate * (1.0 + down * (1.0 - gate))
    point = mm(coarse, wp[...], 0, 0)
    gate = sigmoid(point)
    slope_point[...] = gate * (1.0 + point * (1.0 - gate))


def pick(tables, relation, slot):
    value = tables[0][slot]
    for n in range(1, 4):
        value = jnp.where(relation == n, tables[n][slot], value)
    return value


def reply_kernel(far_slots, own, beside, across, diagonal, reply):
    me = lax.axis_index("brick")
    asked = far_slots[...]
    for i in range(4):
        mine = (asked >> 3) == (me & 4) + i
        slot = jnp.sum(jnp.where(mine, (asked & 7).astype(F32), 0.0)).astype(jnp.int32)
        reply[i] = pick((own, beside, across, diagonal), (me & 3) ^ i, slot)


def near_kernel(slots, own, beside, across, diagonal, near, place):
    me = lax.axis_index("brick")
    for b in range(8):
        target = slots[b] >> 3
        near[b] = pick((own, beside, across, diagonal), (target ^ me) & 3, slots[b] & 7)
        at = jnp.where(((target ^ me) & 4) == 0, -1, target & 3)
        place[b : b + 1, :] = jnp.full((1, 256), at, jnp.int32)


def backward_kernel(
    shifted, slope_pre, hid, coarse, slope_down, slope_point, near, place, far, wd, wp, wire,
    grads,
):
    me = lax.axis_index("brick")
    core = me & 1

    def put(first, value):
        done = 0
        while done < value.shape[0]:
            (stream, half), at = divmod((first + done) // PART, 2), (first + done) % PART
            size = min(value.shape[0] - done, PART - at)
            side = core if half == 0 else 1 - core
            wire[side, stream, at : at + size] = value[done : done + size].astype(BF16)
            done += size

    wanted = []
    for b in range(8):
        value, at = near[b].astype(F32), place[b : b + 1, :]
        for i in range(4):
            value = jnp.where(at == i, far[i].astype(F32), value)
        wanted.append(value)
    parts = [wanted[b][16 * p : 16 * p + 16] for p in range(4) for b in range(8)]
    cot_rows = jnp.concatenate(parts, axis=0)
    grad_point = (cot_rows * slope_point[...]).astype(BF16)
    gwp = mm(coarse[...], grad_point)
    put(POINT_AT, gwp[:, :128])
    put(POINT_AT + 128, gwp[:, 128:])
    grad_coarse = mm(wp[...], grad_point, 1, 1).astype(BF16)
    grad_down = (grad_coarse.astype(F32) * slope_down[...]).astype(BF16)
    put(0, mm(hid[...], grad_down, 1, 1))
    for jk in range(4):
        grad_hidden = mm(wd[128 * jk : 128 * jk + 128], grad_down)
        for p in range(4):
            cut = slice(128 * jk, 128 * jk + 128)
            value = grad_hidden[:, 128 * p : 128 * p + 128] * slope_pre[128 * p : 128 * p + 128, cut]
            h, base = p // 2, 128 * (p % 2)
            grads[base : base + 128, 512 * h + 128 * jk : 512 * h + 128 * jk + 128] = value.astype(BF16)
    low_lanes = lax.broadcasted_iota(jnp.int32, (64, 128), 1) < 64
    thirds = []
    for n in range(9):
        b, c = divmod(n, 3)
        left = jnp.concatenate(
            [
                shifted[j + b, 256 * h : 256 * h + 384, 128 * c : 128 * c + 256]
                for h in range(2)
                for j in range(2)
            ],
            axis=1,
        )
        band = mm(left, grads[...], 1, 1)
        sums = []
        for a in range(3):
            even = band[64 * a : 64 * a + 64, :128] + band[64 * a + 128 : 64 * a + 192, 128:]
            odd = band[64 * a + 64 : 64 * a + 128, :128] + band[64 * a + 192 : 64 * a + 256, 128:]
            both = jnp.where(low_lanes, even, odd)
            sums.append(both + pltpu.roll(both, 64, 1))
        put(CONV_AT + 64 * n, jnp.where(low_lanes, sums[0], sums[1]))
        thirds.append(sums[2])
    for n in range(5):
        put(CONV_AT + 64 * (9 + n), jnp.where(low_lanes, thirds[2 * n], thirds[min(2 * n + 1, 8)]))


def finish_kernel(mine_a, other_a, mine_b, other_b, gwc, gwd, gwp):
    def emit(halves):
        def rows(first, count):
            parts = []
            while count:
                (stream, half), at = divmod(first // PART, 2), first % PART
                size = min(count, PART - at)
                parts.append(halves[half][stream][at : at + size].astype(F32))
                first, count = first + size, count - size
            return jnp.concatenate(parts, axis=0) if len(parts) > 1 else parts[0]

        for i in range(2):
            for jk in range(4):
                gwd[4 * i + jk] = rows(128 * jk + 64 * i, 64)
        for n in range(2):
            gwp[:, 128 * n : 128 * n + 128] = rows(POINT_AT + 128 * n, 128)
        for n in range(14):
            pair = rows(CONV_AT + 64 * n, 64)
            first, second = (n, 9 + n) if n < 9 else (2 * n, 2 * n + 1)
            gwc[first] = pair[:, :64]
            if second < 27:
                gwc[second] = pair[:, 64:]

    core = lax.axis_index("brick") & 1
    mine, other = (mine_a, mine_b), (other_a, other_b)
    pl.when(core == 0)(lambda: emit((mine, other)))
    pl.when(core == 1)(lambda: emit((other, mine)))


def call(kernel, outs, ins, scratch=(), limit=24 * 2**20, flops=0, specs=None):
    return pl.pallas_call(
        kernel,
        out_shape=outs,
        in_specs=specs or [VMEM] * len(ins),
        out_specs=jax.tree.map(lambda _: VMEM, outs),
        scratch_shapes=scratch,
        compiler_params=pltpu.CompilerParams(vmem_limit_bytes=limit),
        cost_estimate=pl.CostEstimate(flops=flops, bytes_accessed=2**20, transcendentals=0),
    )(*ins)


def in_hbm(*arrays):
    return [pltpu.with_memory_space_constraint(array, pltpu.HBM) for array in arrays]


def swap(value, axis, bit):
    size = lax.axis_size(axis)
    return lax.ppermute(value, axis, [(i, i ^ bit) for i in range(size)])


def powers(size, first):
    bits = []
    while first < size:
        bits.append(first)
        first *= 2
    return bits


def shards(features, occupancy, neighbours, owners, w_conv, w_down, w_point, cotangent):
    brick_size = lax.axis_size("brick")
    shape = jax.ShapeDtypeStruct
    core = lax.axis_index("brick") & 1
    split = brick_size == 8
    feat = jnp.swapaxes(features[0], 1, 2)
    slots, own = owners[0], cotangent[0]
    first, last = feat[0:4, :, 0:128], feat[4:8, :, 384:512]
    beside = swap(jnp.where(core == 0, last, first), "brick", 1)
    chips = [(i, i + 1) for i in range(1, brick_size - 1, 2)]
    across = lax.ppermute(jnp.where(core == 0, first, last), "brick", chips + [(j, i) for i, j in chips])
    arguments = (feat, occupancy[0], neighbours[0], w_conv.reshape(27, 64, 64), w_down.reshape(8, 64, 128), w_point)
    planes, occ_x, valid, wide, wd, wp, own_copy, slots_copy = call(
        prepare_kernel,
        (
            shape((512, 512), BF16),
            shape((8, 512), F32),
            shape((27, 128), F32),
            shape((256, 3456), BF16),
            shape((512, 128), BF16),
            shape((128, 256), BF16),
            shape((8, 64, 256), BF16),
            shape((8,), jnp.int32),
        ),
        in_hbm(*arguments, own, slots),
        scratch=[
            pltpu.VMEM((8, 64, 512), BF16),
            pltpu.VMEM((8, 512), jnp.int32),
            pltpu.VMEM((8, 27), jnp.int32),
            pltpu.VMEM((27, 64, 64), BF16),
            pltpu.SemaphoreType.DMA((15,)),
        ],
        flops=4 * 10**9,
        specs=[HBM] * 8,
    )
    if split:
        partner, far_slots, planes, beside, across = lax.optimization_barrier(
            (swap(own, "brick", 2), swap(owners, "brick", 4), planes, beside, across)
        )
        tables = (own_copy, swap(own, "brick", 1), partner, swap(partner, "brick", 1))
        reply = call(reply_kernel, shape((4, 64, 256), BF16), (far_slots, *tables))
        near, place = call(
            near_kernel,
            (shape((8, 64, 256), BF16), shape((8, 256), jnp.int32)),
            (slots_copy, *tables),
            specs=[SMEM] + [VMEM] * 4,
        )
        far = swap(reply, "brick", 4)
    else:
        wanted = jnp.arange(brick_size, dtype=jnp.int32)[:, None] == (slots >> 3)[None, :]
        request = jnp.max(jnp.where(wanted, (slots & 7)[None, :], 0), axis=1)
        arrived = lax.all_to_all(request, "brick", split_axis=0, concat_axis=0, tiled=True)
        reply = jnp.take(own, arrived, axis=0, mode="clip")
        fetched = lax.all_to_all(reply, "brick", split_axis=0, concat_axis=0, tiled=True)
        near = jnp.take(fetched, slots >> 3, axis=0, mode="clip")
        far, place = near[:4], jnp.full((8, 256), -1, jnp.int32)
    saved = call(
        forward_kernel,
        (
            shape((4, 640, 512), BF16),
            shape((512, 512), F32),
            shape((512, 512), BF16),
            shape((128, 512), BF16),
            shape((128, 512), F32),
            shape((512, 256), F32),
        ),
        (planes, occ_x, valid, beside, across, wide, wd, wp),
        scratch=[pltpu.VMEM((640, 512), BF16)],
        flops=4 * 10**9,
    )
    wire = call(
        backward_kernel,
        shape((2, 2, PART, 128), BF16),
        (*saved, near, place, far, wd, wp),
        scratch=[pltpu.VMEM((256, 1024), BF16)],
        flops=4 * 10**9,
    )
    far_steps = [("brick", bit) for bit in powers(brick_size, 4)]
    x, y, z = [("dp", 1)], [("dp", 2)], [("brick", 2)]
    orders = z + x + y + far_steps, x + y + far_steps + z
    sums = [wire[0, n] + swap(wire[1, n], "brick", 1) for n in range(2)]
    for n in range(len(orders[0])):
        for stream in range(2):
            sums[stream] = sums[stream] + swap(sums[stream], *orders[stream][n])
    others = [swap(total, "brick", 1) for total in sums]
    gwc, gwd, gwp = call(
        finish_kernel,
        (shape((27, 64, 64), F32), shape((8, 64, 128), F32), shape((128, 256), F32)),
        (sums[0], others[0], sums[1], others[1]),
    )
    return gwc.reshape(3, 3, 3, 64, 64), gwd.reshape(2, 2, 2, 64, 128), gwp


def solution(mesh):
    in_specs = (
        P("dp", "brick", None, None),
        P("dp", "brick", None),
        P("dp", "brick", None),
        P("dp", "brick"),
        P(),
        P(),
        P(),
        P("dp", "brick", None, None),
    )
    out_specs = (P(), P(), P())
    return jax.shard_map(shards, mesh=mesh, in_specs=in_specs, out_specs=out_specs, check_vma=False)
```

```python
import functools

import jax
import jax.numpy as jnp
from jax import lax
from jax.experimental import pallas as pl
from jax.experimental.pallas import tpu as pltpu
from jax.sharding import PartitionSpec as P

F32 = jnp.float32
BF16 = jnp.bfloat16
LANES = 128
VMEM = pl.BlockSpec(memory_space=pltpu.VMEM)
HBM = pl.BlockSpec(memory_space=pltpu.HBM)
SMEM = pl.BlockSpec(memory_space=pltpu.SMEM)
POINT_AT, CONV_AT = 512, 768
PART = 416


def mm(a, b, ca=1, cb=0):
    return lax.dot_general(a, b, (((ca,), (cb,)), ((), ())), preferred_element_type=F32)


def sigmoid(v):
    return 1.0 / (1.0 + jnp.exp(-v))


def turned_weights(w_conv):
    near = lax.broadcasted_iota(jnp.int32, (64, 64), 0) == lax.broadcasted_iota(jnp.int32, (64, 64), 1)
    eye = jnp.where(near, 1.0, 0.0).astype(BF16)
    zero = jnp.zeros((64, 64), BF16)
    first = jnp.concatenate([w_conv[9 * a + n] if a < 3 else zero for n in range(9) for a in range(4)], axis=0)
    second = jnp.concatenate([w_conv[9 * a + n] if a >= 0 else zero for n in range(9) for a in range(-1, 3)], axis=0)
    return mm(eye, first, 1, 1).astype(BF16), mm(eye, second, 1, 1).astype(BF16)


def near_masks(neighbours):
    brick = lax.broadcasted_iota(jnp.int32, (8, 128), 0)
    lane = lax.broadcasted_iota(jnp.int32, (8, 128), 1)
    spread = jnp.where(lane // 16 == brick, 1.0, 0.0)
    return mm(jnp.where(neighbours >= 0, 1.0, 0.0), spread, 0, 0)


def shift_planes(planes, valid, shifted):
    cell = lax.broadcasted_iota(jnp.int32, (1, 128), 1)
    q_at, r_at = cell // 4 % 4, cell % 4
    source = ((1, -1), (0, 0), (1, 0), (0, 1))
    for t in range(4):
        j, dq = source[t]
        for u in range(4):
            k, dr = source[u]
            g = 2 * j + k
            block = planes[:, 128 * g : 128 * g + 128]
            shift = -(4 * dq + dr) % 128
            if shift:
                block = pltpu.roll(block, shift, 1)
            if dr:
                inside = jnp.where((r_at + dr < 0) | (r_at + dr > 3), 0.0, 1.0)
            else:
                inside = jnp.ones((1, 128), F32)
            cross = None if dq == 0 else (q_at == 0 if dq < 0 else q_at == 3)
            for a, (lo, hi) in enumerate(((0, 64), (64, 576), (576, 640))):
                keep = inside
                near = valid[9 * a + 4 : 9 * a + 5]
                if cross is not None:
                    col = 9 * a + 3 * (dq + 1) + 1
                    keep = keep * jnp.where(cross, valid[col : col + 1], near)
                elif a != 1:
                    keep = keep * near
                part = block[lo:hi]
                if a != 1 or dq or dr:
                    part = part * keep.astype(part.dtype)
                shifted[t, lo:hi, 128 * u : 128 * u + 128] = part.astype(BF16)


def voxel_at():
    lane = lax.broadcasted_iota(jnp.int32, (1, 512), 1)
    jj, kk, bb, qq, rr = lane // 256, lane // 128 % 2, lane % 128 // 16, lane // 4 % 4, lane % 4
    return bb * 128 + 8 * (2 * qq + jj) + 2 * rr + kk


def prepare_kernel(
    feat_hbm, occ_hbm, neighbours_hbm, w_conv_hbm, wd_hbm, wp_hbm, own_hbm, slots_hbm,
    planes, occ_x, valid, wide, wd_rows, wp, own, slots,
    feat, occ, neighbours, w_conv, sems,
):
    pairs = [(w_conv_hbm, w_conv), (feat_hbm, feat), (occ_hbm, occ), (neighbours_hbm, neighbours)]
    pairs += [(wp_hbm, wp), (own_hbm, own), (slots_hbm, slots)]
    for jk in range(4):
        for i in range(2):
            n = 2 * jk + i
            pairs.append((wd_hbm.at[4 * i + jk], wd_rows.at[64 * n : 64 * n + 64]))
    copies = [pltpu.make_async_copy(source, target, sems.at[n]) for n, (source, target) in enumerate(pairs)]
    for copy in copies:
        copy.start()
    copies[0].wait()
    first, second = turned_weights(w_conv)
    zero = jnp.zeros((64, 128), BF16)
    for n in range(9):
        cut = slice(256 * n, 256 * n + 256)
        for x in range(4):
            band = (first if x % 2 == 0 else second)[:, cut]
            band = [band, zero] if x < 2 else [zero, band]
            wide[64 * x : 64 * x + 64, 384 * n : 384 * n + 384] = jnp.concatenate(band, axis=1)
    voxel = voxel_at()
    row = lax.broadcasted_iota(jnp.int32, (1024, 512), 0)
    copies[1].wait()
    copies[2].wait()
    occ_f = occ[...].astype(F32).astype(BF16)
    rows = []
    for m in range(4):
        rows.append(jnp.concatenate([feat[b, :, 128 * m : 128 * m + 128] for b in range(8)], axis=1))
    occ_rows = [
        jnp.concatenate([occ_f[b : b + 1, 128 * m : 128 * m + 128] for b in range(8)], axis=1)
        for m in range(4)
    ]
    occ_rows = jnp.concatenate(occ_rows + [jnp.zeros((12, 1024), BF16)], axis=0)
    stacked = jnp.concatenate(rows + [occ_rows], axis=0)
    for e in range(2):
        select = jnp.where(row == voxel + 64 * e, 1.0, 0.0).astype(BF16)
        picked = mm(stacked, select)
        for m in range(4):
            planes[64 * (2 * m + e) : 64 * (2 * m + e + 1), :] = picked[64 * m : 64 * m + 64].astype(BF16)
            occ_x[2 * m + e : 2 * m + e + 1] = picked[256 + m : 257 + m]
    copies[3].wait()
    valid[...] = near_masks(neighbours[...])
    for copy in copies[4:]:
        copy.wait()


def forward_kernel(
    inner, occ_x, valid, beside, across, wide, wd, wp,
    shifted, slope_pre, hid, coarse_ref, slope_down, slope_point,
    planes,
):
    planes[64:576] = inner[...]
    odd_core = lax.axis_index("brick") & 1 == 1
    inner_x = lax.broadcasted_iota(jnp.int32, (64, 128), 1) >= 64
    row = lax.broadcasted_iota(jnp.int32, (512, 512), 0)
    before = jnp.concatenate([jnp.where(odd_core, beside[b], across[b]) for b in range(4)], axis=1)
    after = jnp.concatenate([jnp.where(odd_core, across[b], beside[b]) for b in range(4)], axis=1)
    before = mm(before, jnp.where(row == voxel_at() - 448, 1.0, 0.0).astype(BF16)).astype(BF16)
    after = mm(after, jnp.where(row == voxel_at(), 1.0, 0.0).astype(BF16)).astype(BF16)
    for g in range(4):
        cut = slice(128 * g, 128 * g + 128)
        planes[0:64, cut] = pltpu.roll(jnp.where(inner_x, before[:, cut], inner[448:512, cut]), 64, 1)
        planes[576:640, cut] = pltpu.roll(jnp.where(inner_x, inner[0:64, cut], after[:, cut]), 64, 1)
    shift_planes(planes, valid, shifted)
    for h in range(2):
        for j in range(2):
            taps = [
                shifted[j + b, 256 * h : 256 * h + 384, 128 * c : 128 * c + 256]
                for b in range(3)
                for c in range(3)
            ]
            pre = mm(wide[...], jnp.concatenate(taps, axis=0))
            gate = sigmoid(pre)
            for x in range(4):
                sub = slice(64 * x, 64 * x + 64)
                filled = occ_x[4 * h + x : 4 * h + x + 1, 256 * j : 256 * j + 256]
                act, g = pre[sub], gate[sub]
                r0 = 256 * h + 64 * x
                slope_pre[r0 : r0 + 64, 256 * j : 256 * j + 256] = filled * (g * (1.0 + act * (1.0 - g)))
                out = (act * g * filled).astype(BF16)
                p, i = 2 * h + x // 2, x % 2
                for k in range(2):
                    base = 128 * (2 * j + k) + 64 * i
                    hid[base : base + 64, 128 * p : 128 * p + 128] = out[:, 128 * k : 128 * k + 128]
    down = mm(wd[...], hid[...], 0, 0)
    gate = sigmoid(down)
    coarse = (down * gate).astype(BF16)
    coarse_ref[...] = coarse
    slope_down[...] = gate * (1.0 + down * (1.0 - gate))
    point = mm(coarse, wp[...], 0, 0)
    gate = sigmoid(point)
    slope_point[...] = gate * (1.0 + point * (1.0 - gate))


def pick(tables, relation, slot):
    value = tables[0][slot]
    for n in range(1, 4):
        value = jnp.where(relation == n, tables[n][slot], value)
    return value


def reply_kernel(chip, far_slots, even, odd, reply):
    me = lax.axis_index("brick")
    asked = far_slots[...]
    for k in range(2):
        mine = (asked >> 3) == (me & 4) + ((me & 2) ^ chip) + k
        slot = jnp.sum(jnp.where(mine, (asked & 7).astype(F32), 0.0)).astype(jnp.int32)
        reply[k] = jnp.where((me & 1) == k, even[slot], odd[slot])


def near_kernel(slots, own, beside, across, diagonal, near, place):
    me = lax.axis_index("brick")
    for b in range(8):
        target = slots[b] >> 3
        near[b] = pick((own, beside, across, diagonal), (target ^ me) & 3, slots[b] & 7)
        at = jnp.where(((target ^ me) & 4) == 0, -1, (target & 3) ^ (me & 2))
        place[b : b + 1, :] = jnp.full((1, 256), at, jnp.int32)


def backward_kernel(
    shifted, slope_pre, hid, coarse, slope_down, slope_point, near, place, far, far_pair, wd, wp, wire,
    grads,
):
    me = lax.axis_index("brick")
    core = me & 1

    def put(first, value):
        done = 0
        while done < value.shape[0]:
            (stream, half), at = divmod((first + done) // PART, 2), (first + done) % PART
            size = min(value.shape[0] - done, PART - at)
            side = core if half == 0 else 1 - core
            wire[side, stream, at : at + size] = value[done : done + size].astype(BF16)
            done += size

    wanted = []
    for b in range(8):
        value, at = near[b].astype(F32), place[b : b + 1, :]
        for i, other in enumerate((far[0], far[1], far_pair[0], far_pair[1])):
            value = jnp.where(at == i, other.astype(F32), value)
        wanted.append(value)
    parts = [wanted[b][16 * p : 16 * p + 16] for p in range(4) for b in range(8)]
    cot_rows = jnp.concatenate(parts, axis=0)
    grad_point = (cot_rows * slope_point[...]).astype(BF16)
    gwp = mm(coarse[...], grad_point)
    put(POINT_AT, gwp[:, :128])
    put(POINT_AT + 128, gwp[:, 128:])
    grad_coarse = mm(wp[...], grad_point, 1, 1).astype(BF16)
    grad_down = (grad_coarse.astype(F32) * slope_down[...]).astype(BF16)
    put(0, mm(hid[...], grad_down, 1, 1))
    for jk in range(4):
        grad_hidden = mm(wd[128 * jk : 128 * jk + 128], grad_down)
        for p in range(4):
            cut = slice(128 * jk, 128 * jk + 128)
            value = grad_hidden[:, 128 * p : 128 * p + 128] * slope_pre[128 * p : 128 * p + 128, cut]
            h, base = p // 2, 128 * (p % 2)
            grads[base : base + 128, 512 * h + 128 * jk : 512 * h + 128 * jk + 128] = value.astype(BF16)
    low_lanes = lax.broadcasted_iota(jnp.int32, (64, 128), 1) < 64
    thirds = []
    for n in range(9):
        b, c = divmod(n, 3)
        left = jnp.concatenate(
            [
                shifted[j + b, 256 * h : 256 * h + 384, 128 * c : 128 * c + 256]
                for h in range(2)
                for j in range(2)
            ],
            axis=1,
        )
        band = mm(left, grads[...], 1, 1)
        sums = []
        for a in range(3):
            even = band[64 * a : 64 * a + 64, :128] + band[64 * a + 128 : 64 * a + 192, 128:]
            odd = band[64 * a + 64 : 64 * a + 128, :128] + band[64 * a + 192 : 64 * a + 256, 128:]
            both = jnp.where(low_lanes, even, odd)
            sums.append(both + pltpu.roll(both, 64, 1))
        put(CONV_AT + 64 * n, jnp.where(low_lanes, sums[0], sums[1]))
        thirds.append(sums[2])
    for n in range(5):
        put(CONV_AT + 64 * (9 + n), jnp.where(low_lanes, thirds[2 * n], thirds[min(2 * n + 1, 8)]))


def finish_kernel(mine_a, other_a, mine_b, other_b, gwc, gwd, gwp):
    def emit(halves):
        def rows(first, count):
            parts = []
            while count:
                (stream, half), at = divmod(first // PART, 2), first % PART
                size = min(count, PART - at)
                parts.append(halves[half][stream][at : at + size].astype(F32))
                first, count = first + size, count - size
            return jnp.concatenate(parts, axis=0) if len(parts) > 1 else parts[0]

        for i in range(2):
            for jk in range(4):
                gwd[4 * i + jk] = rows(128 * jk + 64 * i, 64)
        for n in range(2):
            gwp[:, 128 * n : 128 * n + 128] = rows(POINT_AT + 128 * n, 128)
        for n in range(14):
            pair = rows(CONV_AT + 64 * n, 64)
            first, second = (n, 9 + n) if n < 9 else (2 * n, 2 * n + 1)
            gwc[first] = pair[:, :64]
            if second < 27:
                gwc[second] = pair[:, 64:]

    core = lax.axis_index("brick") & 1
    mine, other = (mine_a, mine_b), (other_a, other_b)
    pl.when(core == 0)(lambda: emit((mine, other)))
    pl.when(core == 1)(lambda: emit((other, mine)))


def call(kernel, outs, ins, scratch=(), limit=24 * 2**20, flops=0, specs=None):
    return pl.pallas_call(
        kernel,
        out_shape=outs,
        in_specs=specs or [VMEM] * len(ins),
        out_specs=jax.tree.map(lambda _: VMEM, outs),
        scratch_shapes=scratch,
        compiler_params=pltpu.CompilerParams(vmem_limit_bytes=limit),
        cost_estimate=pl.CostEstimate(flops=flops, bytes_accessed=2**20, transcendentals=0),
    )(*ins)


def in_hbm(*arrays):
    return [pltpu.with_memory_space_constraint(array, pltpu.HBM) for array in arrays]


def swap(value, axis, bit):
    size = lax.axis_size(axis)
    return lax.ppermute(value, axis, [(i, i ^ bit) for i in range(size)])


def powers(size, first):
    bits = []
    while first < size:
        bits.append(first)
        first *= 2
    return bits


def shards(features, occupancy, neighbours, owners, w_conv, w_down, w_point, cotangent):
    brick_size = lax.axis_size("brick")
    shape = jax.ShapeDtypeStruct
    core = lax.axis_index("brick") & 1
    split = brick_size == 8
    feat = jnp.swapaxes(features[0], 1, 2)
    slots, own = owners[0], cotangent[0]
    first, last = feat[0:4, :, 0:128], feat[4:8, :, 384:512]
    beside = swap(jnp.where(core == 0, last, first), "brick", 1)
    chips = [(i, i + 1) for i in range(1, brick_size - 1, 2)]
    across = lax.ppermute(jnp.where(core == 0, first, last), "brick", chips + [(j, i) for i, j in chips])
    arguments = (feat, occupancy[0], neighbours[0], w_conv.reshape(27, 64, 64), w_down.reshape(8, 64, 128), w_point)
    planes, occ_x, valid, wide, wd, wp, own_copy, slots_copy = call(
        prepare_kernel,
        (
            shape((512, 512), BF16),
            shape((8, 512), F32),
            shape((27, 128), F32),
            shape((256, 3456), BF16),
            shape((512, 128), BF16),
            shape((128, 256), BF16),
            shape((8, 64, 256), BF16),
            shape((8,), jnp.int32),
        ),
        in_hbm(*arguments, own, slots),
        scratch=[
            pltpu.VMEM((8, 64, 512), BF16),
            pltpu.VMEM((8, 512), jnp.int32),
            pltpu.VMEM((8, 27), jnp.int32),
            pltpu.VMEM((27, 64, 64), BF16),
            pltpu.SemaphoreType.DMA((15,)),
        ],
        flops=4 * 10**9,
        specs=[HBM] * 8,
    )
    if split:
        partner, far_slots, planes, beside, across = lax.optimization_barrier(
            (swap(own, "brick", 2), swap(owners, "brick", 4), planes, beside, across)
        )
        tables = (own_copy, swap(own, "brick", 1), partner, swap(partner, "brick", 1))
        fars = []
        for chip in (0, 2):
            kernel = functools.partial(reply_kernel, chip)
            reply = call(kernel, shape((2, 64, 256), BF16), (far_slots, *tables[chip : chip + 2]))
            fars.append(swap(reply, "brick", 4))
        near, place = call(
            near_kernel,
            (shape((8, 64, 256), BF16), shape((8, 256), jnp.int32)),
            (slots_copy, *tables),
            specs=[SMEM] + [VMEM] * 4,
        )
    else:
        wanted = jnp.arange(brick_size, dtype=jnp.int32)[:, None] == (slots >> 3)[None, :]
        request = jnp.max(jnp.where(wanted, (slots & 7)[None, :], 0), axis=1)
        arrived = lax.all_to_all(request, "brick", split_axis=0, concat_axis=0, tiled=True)
        reply = jnp.take(own, arrived, axis=0, mode="clip")
        fetched = lax.all_to_all(reply, "brick", split_axis=0, concat_axis=0, tiled=True)
        near = jnp.take(fetched, slots >> 3, axis=0, mode="clip")
        fars, place = [near[:2], near[2:4]], jnp.full((8, 256), -1, jnp.int32)
    saved = call(
        forward_kernel,
        (
            shape((4, 640, 512), BF16),
            shape((512, 512), F32),
            shape((512, 512), BF16),
            shape((128, 512), BF16),
            shape((128, 512), F32),
            shape((512, 256), F32),
        ),
        (planes, occ_x, valid, beside, across, wide, wd, wp),
        scratch=[pltpu.VMEM((640, 512), BF16)],
        flops=4 * 10**9,
    )
    wire = call(
        backward_kernel,
        shape((2, 2, PART, 128), BF16),
        (*saved, near, place, *fars, wd, wp),
        scratch=[pltpu.VMEM((256, 1024), BF16)],
        flops=4 * 10**9,
    )
    far_steps = [("brick", bit) for bit in powers(brick_size, 4)]
    x, y, z = [("dp", 1)], [("dp", 2)], [("brick", 2)]
    orders = z + x + y + far_steps, x + y + far_steps + z
    sums = [wire[0, n] + swap(wire[1, n], "brick", 1) for n in range(2)]
    for n in range(len(orders[0])):
        for stream in range(2):
            sums[stream] = sums[stream] + swap(sums[stream], *orders[stream][n])
    others = [swap(total, "brick", 1) for total in sums]
    gwc, gwd, gwp = call(
        finish_kernel,
        (shape((27, 64, 64), F32), shape((8, 64, 128), F32), shape((128, 256), F32)),
        (sums[0], others[0], sums[1], others[1]),
    )
    return gwc.reshape(3, 3, 3, 64, 64), gwd.reshape(2, 2, 2, 64, 128), gwp


def solution(mesh):
    in_specs = (
        P("dp", "brick", None, None),
        P("dp", "brick", None),
        P("dp", "brick", None),
        P("dp", "brick"),
        P(),
        P(),
        P(),
        P("dp", "brick", None, None),
    )
    out_specs = (P(), P(), P())
    return jax.shard_map(shards, mesh=mesh, in_specs=in_specs, out_specs=out_specs, check_vma=False)
```

```python
import functools

import jax
import jax.numpy as jnp
from jax import lax
from jax.experimental import pallas as pl
from jax.experimental.pallas import tpu as pltpu
from jax.sharding import PartitionSpec as P

F32 = jnp.float32
BF16 = jnp.bfloat16
LANES = 128
VMEM = pl.BlockSpec(memory_space=pltpu.VMEM)
HBM = pl.BlockSpec(memory_space=pltpu.HBM)
SMEM = pl.BlockSpec(memory_space=pltpu.SMEM)
POINT_AT, CONV_AT = 512, 768
PART = 416


def mm(a, b, ca=1, cb=0):
    return lax.dot_general(a, b, (((ca,), (cb,)), ((), ())), preferred_element_type=F32)


def sigmoid(v):
    return 1.0 / (1.0 + jnp.exp(-v))


def turned_weights(w_conv):
    near = lax.broadcasted_iota(jnp.int32, (64, 64), 0) == lax.broadcasted_iota(jnp.int32, (64, 64), 1)
    eye = jnp.where(near, 1.0, 0.0).astype(BF16)
    zero = jnp.zeros((64, 64), BF16)
    first = jnp.concatenate([w_conv[9 * a + n] if a < 3 else zero for n in range(9) for a in range(4)], axis=0)
    second = jnp.concatenate([w_conv[9 * a + n] if a >= 0 else zero for n in range(9) for a in range(-1, 3)], axis=0)
    return mm(eye, first, 1, 1).astype(BF16), mm(eye, second, 1, 1).astype(BF16)


def near_masks(neighbours):
    brick = lax.broadcasted_iota(jnp.int32, (8, 128), 0)
    lane = lax.broadcasted_iota(jnp.int32, (8, 128), 1)
    spread = jnp.where(lane // 16 == brick, 1.0, 0.0)
    return mm(jnp.where(neighbours >= 0, 1.0, 0.0), spread, 0, 0)


def shift_planes(planes, valid, shifted):
    cell = lax.broadcasted_iota(jnp.int32, (1, 128), 1)
    q_at, r_at = cell // 4 % 4, cell % 4
    source = ((1, -1), (0, 0), (1, 0), (0, 1))
    for t in range(4):
        j, dq = source[t]
        for u in range(4):
            k, dr = source[u]
            g = 2 * j + k
            block = planes[:, 128 * g : 128 * g + 128]
            shift = -(4 * dq + dr) % 128
            if shift:
                block = pltpu.roll(block, shift, 1)
            if dr:
                inside = jnp.where((r_at + dr < 0) | (r_at + dr > 3), 0.0, 1.0)
            else:
                inside = jnp.ones((1, 128), F32)
            cross = None if dq == 0 else (q_at == 0 if dq < 0 else q_at == 3)
            for a, (lo, hi) in enumerate(((0, 64), (64, 576), (576, 640))):
                keep = inside
                near = valid[9 * a + 4 : 9 * a + 5]
                if cross is not None:
                    col = 9 * a + 3 * (dq + 1) + 1
                    keep = keep * jnp.where(cross, valid[col : col + 1], near)
                elif a != 1:
                    keep = keep * near
                part = block[lo:hi]
                if a != 1 or dq or dr:
                    part = part * keep.astype(part.dtype)
                shifted[t, lo:hi, 128 * u : 128 * u + 128] = part.astype(BF16)


def voxel_at():
    lane = lax.broadcasted_iota(jnp.int32, (1, 512), 1)
    jj, kk, bb, qq, rr = lane // 256, lane // 128 % 2, lane % 128 // 16, lane // 4 % 4, lane % 4
    return bb * 128 + 8 * (2 * qq + jj) + 2 * rr + kk


def prepare_kernel(
    feat_hbm, occ_hbm, neighbours_hbm, w_conv_hbm, wd_hbm, wp_hbm, own_hbm, slots_hbm,
    planes, occ_x, valid, wide, wd_rows, wp, own, slots,
    feat, occ, neighbours, w_conv, sems,
):
    pairs = [(w_conv_hbm, w_conv), (feat_hbm, feat), (occ_hbm, occ), (neighbours_hbm, neighbours)]
    pairs += [(wp_hbm, wp), (own_hbm, own), (slots_hbm, slots)]
    for jk in range(4):
        for i in range(2):
            n = 2 * jk + i
            pairs.append((wd_hbm.at[4 * i + jk], wd_rows.at[64 * n : 64 * n + 64]))
    copies = [pltpu.make_async_copy(source, target, sems.at[n]) for n, (source, target) in enumerate(pairs)]
    for copy in copies:
        copy.start()
    copies[0].wait()
    first, second = turned_weights(w_conv)
    zero = jnp.zeros((64, 128), BF16)
    for n in range(9):
        cut = slice(256 * n, 256 * n + 256)
        for x in range(4):
            band = (first if x % 2 == 0 else second)[:, cut]
            band = [band, zero] if x < 2 else [zero, band]
            wide[64 * x : 64 * x + 64, 384 * n : 384 * n + 384] = jnp.concatenate(band, axis=1)
    voxel = voxel_at()
    row = lax.broadcasted_iota(jnp.int32, (1024, 512), 0)
    copies[1].wait()
    copies[2].wait()
    occ_f = occ[...].astype(F32).astype(BF16)
    rows = []
    for m in range(4):
        rows.append(jnp.concatenate([feat[b, :, 128 * m : 128 * m + 128] for b in range(8)], axis=1))
    occ_rows = [
        jnp.concatenate([occ_f[b : b + 1, 128 * m : 128 * m + 128] for b in range(8)], axis=1)
        for m in range(4)
    ]
    occ_rows = jnp.concatenate(occ_rows + [jnp.zeros((12, 1024), BF16)], axis=0)
    stacked = jnp.concatenate(rows + [occ_rows], axis=0)
    for e in range(2):
        select = jnp.where(row == voxel + 64 * e, 1.0, 0.0).astype(BF16)
        picked = mm(stacked, select)
        for m in range(4):
            planes[64 * (2 * m + e) : 64 * (2 * m + e + 1), :] = picked[64 * m : 64 * m + 64].astype(BF16)
            occ_x[2 * m + e : 2 * m + e + 1] = picked[256 + m : 257 + m]
    copies[3].wait()
    valid[...] = near_masks(neighbours[...])
    for copy in copies[4:]:
        copy.wait()


def forward_kernel(
    inner, occ_x, valid, beside, across, wide, wd, wp,
    shifted, slope_pre, hid, coarse_ref, slope_down, slope_point,
    planes,
):
    planes[64:576] = inner[...]
    odd_core = lax.axis_index("brick") & 1 == 1
    inner_x = lax.broadcasted_iota(jnp.int32, (64, 128), 1) >= 64
    row = lax.broadcasted_iota(jnp.int32, (256, 512), 0)
    voxel = voxel_at()
    voxel = voxel - 64 * (voxel // 128)
    before = jnp.where(odd_core, beside[...], across[...])
    after = jnp.where(odd_core, across[...], beside[...])
    before = mm(before, jnp.where(row == voxel - 256, 1.0, 0.0).astype(BF16)).astype(BF16)
    after = mm(after, jnp.where(row == voxel, 1.0, 0.0).astype(BF16)).astype(BF16)
    for g in range(4):
        cut = slice(128 * g, 128 * g + 128)
        planes[0:64, cut] = pltpu.roll(jnp.where(inner_x, before[:, cut], inner[448:512, cut]), 64, 1)
        planes[576:640, cut] = pltpu.roll(jnp.where(inner_x, inner[0:64, cut], after[:, cut]), 64, 1)
    shift_planes(planes, valid, shifted)
    for h in range(2):
        for j in range(2):
            taps = [
                shifted[j + b, 256 * h : 256 * h + 384, 128 * c : 128 * c + 256]
                for b in range(3)
                for c in range(3)
            ]
            pre = mm(wide[...], jnp.concatenate(taps, axis=0))
            gate = sigmoid(pre)
            for x in range(4):
                sub = slice(64 * x, 64 * x + 64)
                filled = occ_x[4 * h + x : 4 * h + x + 1, 256 * j : 256 * j + 256]
                act, g = pre[sub], gate[sub]
                r0 = 256 * h + 64 * x
                slope_pre[r0 : r0 + 64, 256 * j : 256 * j + 256] = filled * (g * (1.0 + act * (1.0 - g)))
                out = (act * g * filled).astype(BF16)
                p, i = 2 * h + x // 2, x % 2
                for k in range(2):
                    base = 128 * (2 * j + k) + 64 * i
                    hid[base : base + 64, 128 * p : 128 * p + 128] = out[:, 128 * k : 128 * k + 128]
    down = mm(wd[...], hid[...], 0, 0)
    gate = sigmoid(down)
    coarse = (down * gate).astype(BF16)
    coarse_ref[...] = coarse
    slope_down[...] = gate * (1.0 + down * (1.0 - gate))
    point = mm(coarse, wp[...], 0, 0)
    gate = sigmoid(point)
    slope_point[...] = gate * (1.0 + point * (1.0 - gate))


def pick(tables, relation, slot):
    value = tables[0][slot]
    for n in range(1, 4):
        value = jnp.where(relation == n, tables[n][slot], value)
    return value


def reply_kernel(chip, far_slots, even, odd, reply):
    me = lax.axis_index("brick")
    asked = far_slots[...]
    for k in range(2):
        mine = (asked >> 3) == (me & 4) + ((me & 2) ^ chip) + k
        slot = jnp.sum(jnp.where(mine, (asked & 7).astype(F32), 0.0)).astype(jnp.int32)
        reply[k] = jnp.where((me & 1) == k, even[slot], odd[slot])


def near_kernel(slots, own, beside, across, diagonal, near, place):
    me = lax.axis_index("brick")
    for b in range(8):
        target = slots[b] >> 3
        near[b] = pick((own, beside, across, diagonal), (target ^ me) & 3, slots[b] & 7)
        at = jnp.where(((target ^ me) & 4) == 0, -1, (target & 3) ^ (me & 2))
        place[b : b + 1, :] = jnp.full((1, 256), at, jnp.int32)


def backward_kernel(
    shifted, slope_pre, hid, coarse, slope_down, slope_point, near, place, far, far_pair, wd, wp, wire,
    grads,
):
    me = lax.axis_index("brick")
    core = me & 1

    def put(first, value):
        done = 0
        while done < value.shape[0]:
            (stream, half), at = divmod((first + done) // PART, 2), (first + done) % PART
            size = min(value.shape[0] - done, PART - at)
            side = core if half == 0 else 1 - core
            wire[side, stream, at : at + size] = value[done : done + size].astype(BF16)
            done += size

    wanted = []
    for b in range(8):
        value, at = near[b].astype(F32), place[b : b + 1, :]
        for i, other in enumerate((far[0], far[1], far_pair[0], far_pair[1])):
            value = jnp.where(at == i, other.astype(F32), value)
        wanted.append(value)
    parts = [wanted[b][16 * p : 16 * p + 16] for p in range(4) for b in range(8)]
    cot_rows = jnp.concatenate(parts, axis=0)
    grad_point = (cot_rows * slope_point[...]).astype(BF16)
    gwp = mm(coarse[...], grad_point)
    put(POINT_AT, gwp[:, :128])
    put(POINT_AT + 128, gwp[:, 128:])
    grad_coarse = mm(wp[...], grad_point, 1, 1).astype(BF16)
    grad_down = (grad_coarse.astype(F32) * slope_down[...]).astype(BF16)
    put(0, mm(hid[...], grad_down, 1, 1))
    for jk in range(4):
        grad_hidden = mm(wd[128 * jk : 128 * jk + 128], grad_down)
        for p in range(4):
            cut = slice(128 * jk, 128 * jk + 128)
            value = grad_hidden[:, 128 * p : 128 * p + 128] * slope_pre[128 * p : 128 * p + 128, cut]
            h, base = p // 2, 128 * (p % 2)
            grads[base : base + 128, 512 * h + 128 * jk : 512 * h + 128 * jk + 128] = value.astype(BF16)
    low_lanes = lax.broadcasted_iota(jnp.int32, (64, 128), 1) < 64
    thirds = []
    for n in range(9):
        b, c = divmod(n, 3)
        left = jnp.concatenate(
            [
                shifted[j + b, 256 * h : 256 * h + 384, 128 * c : 128 * c + 256]
                for h in range(2)
                for j in range(2)
            ],
            axis=1,
        )
        band = mm(left, grads[...], 1, 1)
        sums = []
        for a in range(3):
            even = band[64 * a : 64 * a + 64, :128] + band[64 * a + 128 : 64 * a + 192, 128:]
            odd = band[64 * a + 64 : 64 * a + 128, :128] + band[64 * a + 192 : 64 * a + 256, 128:]
            both = jnp.where(low_lanes, even, odd)
            sums.append(both + pltpu.roll(both, 64, 1))
        put(CONV_AT + 64 * n, jnp.where(low_lanes, sums[0], sums[1]))
        thirds.append(sums[2])
    for n in range(5):
        put(CONV_AT + 64 * (9 + n), jnp.where(low_lanes, thirds[2 * n], thirds[min(2 * n + 1, 8)]))


def finish_kernel(mine_a, other_a, mine_b, other_b, gwc, gwd, gwp):
    def emit(halves):
        def rows(first, count):
            parts = []
            while count:
                (stream, half), at = divmod(first // PART, 2), first % PART
                size = min(count, PART - at)
                parts.append(halves[half][stream][at : at + size].astype(F32))
                first, count = first + size, count - size
            return jnp.concatenate(parts, axis=0) if len(parts) > 1 else parts[0]

        for i in range(2):
            for jk in range(4):
                gwd[4 * i + jk] = rows(128 * jk + 64 * i, 64)
        for n in range(2):
            gwp[:, 128 * n : 128 * n + 128] = rows(POINT_AT + 128 * n, 128)
        for n in range(14):
            pair = rows(CONV_AT + 64 * n, 64)
            first, second = (n, 9 + n) if n < 9 else (2 * n, 2 * n + 1)
            gwc[first] = pair[:, :64]
            if second < 27:
                gwc[second] = pair[:, 64:]

    core = lax.axis_index("brick") & 1
    mine, other = (mine_a, mine_b), (other_a, other_b)
    pl.when(core == 0)(lambda: emit((mine, other)))
    pl.when(core == 1)(lambda: emit((other, mine)))


def call(kernel, outs, ins, scratch=(), limit=24 * 2**20, flops=0, specs=None):
    return pl.pallas_call(
        kernel,
        out_shape=outs,
        in_specs=specs or [VMEM] * len(ins),
        out_specs=jax.tree.map(lambda _: VMEM, outs),
        scratch_shapes=scratch,
        compiler_params=pltpu.CompilerParams(vmem_limit_bytes=limit),
        cost_estimate=pl.CostEstimate(flops=flops, bytes_accessed=2**20, transcendentals=0),
    )(*ins)


def in_hbm(*arrays):
    return [pltpu.with_memory_space_constraint(array, pltpu.HBM) for array in arrays]


def swap(value, axis, bit):
    size = lax.axis_size(axis)
    return lax.ppermute(value, axis, [(i, i ^ bit) for i in range(size)])


def powers(size, first):
    bits = []
    while first < size:
        bits.append(first)
        first *= 2
    return bits


def shards(features, occupancy, neighbours, owners, w_conv, w_down, w_point, cotangent):
    brick_size = lax.axis_size("brick")
    shape = jax.ShapeDtypeStruct
    core = lax.axis_index("brick") & 1
    split = brick_size == 8
    feat = jnp.swapaxes(features[0], 1, 2)
    slots, own = owners[0], cotangent[0]
    first = jnp.concatenate([feat[b, :, 0:64] for b in range(4)], axis=1)
    last = jnp.concatenate([feat[b, :, 448:512] for b in range(4, 8)], axis=1)
    beside = swap(jnp.where(core == 0, last, first), "brick", 1)
    chips = [(i, i + 1) for i in range(1, brick_size - 1, 2)]
    across = lax.ppermute(jnp.where(core == 0, first, last), "brick", chips + [(j, i) for i, j in chips])
    arguments = (feat, occupancy[0], neighbours[0], w_conv.reshape(27, 64, 64), w_down.reshape(8, 64, 128), w_point)
    planes, occ_x, valid, wide, wd, wp, own_copy, slots_copy = call(
        prepare_kernel,
        (
            shape((512, 512), BF16),
            shape((8, 512), F32),
            shape((27, 128), F32),
            shape((256, 3456), BF16),
            shape((512, 128), BF16),
            shape((128, 256), BF16),
            shape((8, 64, 256), BF16),
            shape((8,), jnp.int32),
        ),
        in_hbm(*arguments, own, slots),
        scratch=[
            pltpu.VMEM((8, 64, 512), BF16),
            pltpu.VMEM((8, 512), jnp.int32),
            pltpu.VMEM((8, 27), jnp.int32),
            pltpu.VMEM((27, 64, 64), BF16),
            pltpu.SemaphoreType.DMA((15,)),
        ],
        flops=4 * 10**9,
        specs=[HBM] * 8,
    )
    if split:
        partner, far_slots, planes, beside, across = lax.optimization_barrier(
            (swap(own, "brick", 2), swap(owners, "brick", 4), planes, beside, across)
        )
        tables = (own_copy, swap(own, "brick", 1), partner, swap(partner, "brick", 1))
        fars = []
        for chip in (0, 2):
            kernel = functools.partial(reply_kernel, chip)
            reply = call(kernel, shape((2, 64, 256), BF16), (far_slots, *tables[chip : chip + 2]))
            fars.append(swap(reply, "brick", 4))
        near, place = call(
            near_kernel,
            (shape((8, 64, 256), BF16), shape((8, 256), jnp.int32)),
            (slots_copy, *tables),
            specs=[SMEM] + [VMEM] * 4,
        )
    else:
        wanted = jnp.arange(brick_size, dtype=jnp.int32)[:, None] == (slots >> 3)[None, :]
        request = jnp.max(jnp.where(wanted, (slots & 7)[None, :], 0), axis=1)
        arrived = lax.all_to_all(request, "brick", split_axis=0, concat_axis=0, tiled=True)
        reply = jnp.take(own, arrived, axis=0, mode="clip")
        fetched = lax.all_to_all(reply, "brick", split_axis=0, concat_axis=0, tiled=True)
        near = jnp.take(fetched, slots >> 3, axis=0, mode="clip")
        fars, place = [near[:2], near[2:4]], jnp.full((8, 256), -1, jnp.int32)
    saved = call(
        forward_kernel,
        (
            shape((4, 640, 512), BF16),
            shape((512, 512), F32),
            shape((512, 512), BF16),
            shape((128, 512), BF16),
            shape((128, 512), F32),
            shape((512, 256), F32),
        ),
        (planes, occ_x, valid, beside, across, wide, wd, wp),
        scratch=[pltpu.VMEM((640, 512), BF16)],
        flops=4 * 10**9,
    )
    wire = call(
        backward_kernel,
        shape((2, 2, PART, 128), BF16),
        (*saved, near, place, *fars, wd, wp),
        scratch=[pltpu.VMEM((256, 1024), BF16)],
        flops=4 * 10**9,
    )
    far_steps = [("brick", bit) for bit in powers(brick_size, 4)]
    x, y, z = [("dp", 1)], [("dp", 2)], [("brick", 2)]
    orders = z + x + y + far_steps, x + y + far_steps + z
    sums = [wire[0, n] + swap(wire[1, n], "brick", 1) for n in range(2)]
    for n in range(len(orders[0])):
        for stream in range(2):
            sums[stream] = sums[stream] + swap(sums[stream], *orders[stream][n])
    others = [swap(total, "brick", 1) for total in sums]
    gwc, gwd, gwp = call(
        finish_kernel,
        (shape((27, 64, 64), F32), shape((8, 64, 128), F32), shape((128, 256), F32)),
        (sums[0], others[0], sums[1], others[1]),
    )
    return gwc.reshape(3, 3, 3, 64, 64), gwd.reshape(2, 2, 2, 64, 128), gwp


def solution(mesh):
    in_specs = (
        P("dp", "brick", None, None),
        P("dp", "brick", None),
        P("dp", "brick", None),
        P("dp", "brick"),
        P(),
        P(),
        P(),
        P("dp", "brick", None, None),
    )
    out_specs = (P(), P(), P())
    return jax.shard_map(shards, mesh=mesh, in_specs=in_specs, out_specs=out_specs, check_vma=False)
```
